128 devices in a mesh: gy: 32 (over y, z, x_lo), gz: 4 (over x_hi, core).
Axes of the slice: x: 4 (x_hi: 2, x_lo: 2; x = x_hi * 2 + x_lo), y: 4, z: 4, core: 2. Of those that a mesh axis runs over, the one named last changes fastest.
Arguments:
- flow_state: bfloat16 [4, 128, 256, 512], P(None, 'gz', 'gy'), may hold values from -4 to 4
- metric: float32 [3, 3], replicated, may hold values from -0.3 to 1.5, as said below
- deformation_matrix: float32 [3, 3], replicated, may hold values from -0.5 to 0.5
Outputs:
- solenoidal_motion: float32 [3, 128, 256, 512], P(None, 'gz', 'gy')
- heat_content_next: float32 [128, 256, 512], P('gz', 'gy')
The draws below stay inside these ranges and needn't reach their ends.
Inputs may be any that keep to these rules, and one draw needn't show every extreme that they name: `metric`: diagonal entries lie between 1 and 1.5, off-diagonal entries have magnitude at most 0.3.
All inputs are finite; a program needn't handle non-finite values.
Results may differ from the reference program's by a relative error of at most 0.0003.
Values may be sent and summed in bfloat16 or wider, within the bound.
No kernel may reach another device: no remote copies, remote signals or barrier semaphores. Data moves between devices by JAX's collectives and lax.ppermute only.
A program may use at most 128 MiB of HBM per device.

```python
import math
import jax
import jax.numpy as jnp

NX = 512
NY = 256
NZ = 128


def draw_flow_state(key, part):
    key = jax.random.fold_in(key, 11)
    extent = (4, NZ, NY, NX)
    values = jnp.clip(jax.random.normal(key, extent, jnp.float32), -4.0, 4.0)
    return values.astype(jnp.bfloat16)


def draw_metric(key, part):
    key = jax.random.fold_in(key, 23)
    leading, second = jax.random.split(key)
    diagonal_top = 1.5
    diagonal_values = jax.random.uniform(leading, (3, 3), jnp.float32, 1.0, diagonal_top)
    outside_values = jax.random.uniform(second, (3, 3), jnp.float32, -0.3, 0.3)
    rows_iota = jnp.arange(3, dtype=jnp.int32)[:, None]
    cols_iota = jnp.arange(3, dtype=jnp.int32)[None, :]
    return jnp.where(rows_iota == cols_iota, diagonal_values, outside_values)


def setup_inputs(seed: int = 0) -> dict:
    seeds = jax.random.split(jax.random.key(seed), 4)
    flow_state = draw_flow_state(jax.random.fold_in(seeds[3], 71), 0)
    metric = draw_metric(jax.random.fold_in(seeds[3], 71), 0)
    deformation_matrix = jnp.clip(jax.random.uniform(seeds[2], (3, 3), jnp.float32, -0.5, 0.5), -0.5, 0.5)
    return dict(flow_state=flow_state, metric=metric, deformation_matrix=deformation_matrix)


substep_width = 0.4
stratification_squared = 1.0


def difference_periodic(forcing_term, along):
    def moved(offset):
        return jnp.roll(forcing_term, -offset, axis=along)
    return (45.0 * (moved(1) - moved(-1)) - 9.0 * (moved(2) - moved(-2)) + (moved(3) - moved(-3))) / 60.0


def wavenumber(modes, length):
    def wave(multiple):
        return jnp.sin((2.0 * math.pi / length) * ((multiple * modes) % length).astype(jnp.float32))
    return 1.5 * wave(1) - 0.3 * wave(2) + wave(3) / 30.0


def reference(flow_state, metric, deformation_matrix):
    state_collection = flow_state.astype(jnp.float32)
    current_speeds = [state_collection[0], state_collection[1], state_collection[2]]
    heat_content = state_collection[3]
    contra = [metric[0, direction] * current_speeds[0] + metric[1, direction] * current_speeds[1] + metric[2, direction] * current_speeds[2] for direction in range(3)]

    def background_stream(forcing_term):
        return contra[0] * difference_periodic(forcing_term, 2) + contra[1] * difference_periodic(forcing_term, 1) + contra[2] * difference_periodic(forcing_term, 0)

    provisional = []
    for vector_entry in range(3):
        evolution_change = -background_stream(current_speeds[vector_entry]) - (deformation_matrix[vector_entry, 0] * current_speeds[0] + deformation_matrix[vector_entry, 1] * current_speeds[1] + deformation_matrix[vector_entry, 2] * current_speeds[2])
        if vector_entry == 2:
            evolution_change = evolution_change + heat_content
        provisional.append(current_speeds[vector_entry] + substep_width * evolution_change)
    heat_content_next = heat_content + substep_width * (-background_stream(heat_content) - stratification_squared * current_speeds[2])
    flow_compressibility = jnp.zeros_like(heat_content)
    for vector_entry in range(3):
        flow_compressibility = flow_compressibility + metric[vector_entry, 0] * difference_periodic(provisional[vector_entry], 2) + metric[vector_entry, 1] * difference_periodic(provisional[vector_entry], 1) + metric[vector_entry, 2] * difference_periodic(provisional[vector_entry], 0)
    spectrum = jnp.fft.fftn(flow_compressibility)
    modes_z = jnp.arange(NZ, dtype=jnp.int32)[:, None, None]
    modes_y = jnp.arange(NY, dtype=jnp.int32)[None, :, None]
    modes_x = jnp.arange(NX, dtype=jnp.int32)[None, None, :]
    waves = [wavenumber(modes_x, NX), wavenumber(modes_y, NY), wavenumber(modes_z, NZ)]
    symbol = jnp.zeros((NZ, NY, NX), jnp.float32)
    for vector_entry in range(3):
        mixed = metric[vector_entry, 0] * waves[0] + metric[vector_entry, 1] * waves[1] + metric[vector_entry, 2] * waves[2]
        symbol = symbol + mixed * mixed
    edge = ((2 * modes_x) % NX == 0) & ((2 * modes_y) % NY == 0) & ((2 * modes_z) % NZ == 0)
    pressure_hat = jnp.where(edge, 0.0, -spectrum / jnp.where(edge, 1.0, symbol))
    pressure = jnp.real(jnp.fft.ifftn(pressure_hat))
    push_x = difference_periodic(pressure, 2)
    push_y = difference_periodic(pressure, 1)
    push_z = difference_periodic(pressure, 0)
    solenoidal_motion = jnp.stack([provisional[vector_entry] - (metric[vector_entry, 0] * push_x + metric[vector_entry, 1] * push_y + metric[vector_entry, 2] * push_z) for vector_entry in range(3)])
    return solenoidal_motion, heat_content_next
```

```python
import numpy as np

import jax
import jax.numpy as jnp
import ml_dtypes
from jax import lax
from jax.experimental import pallas as pl
from jax.experimental.pallas import tpu as pltpu
from jax.sharding import PartitionSpec as P

F32 = jnp.float32
BF16 = jnp.bfloat16
NX, NY, NZ = 512, 256, 128
GY, GZ = 32, 4
BY, BZ = NY // GY, NZ // GZ
DEV = GY * GZ
CELLS = BY * BZ
EXT = 512
STEP = 0.4
COEF = {1: 45.0, -1: -45.0, 2: -9.0, -2: 9.0, 3: 1.0, -3: -1.0}
MIB = 1 << 20


def _pieces(table, count):
    rest = np.asarray(table, np.float64)
    out = []
    for _ in range(count):
        piece = rest.astype(np.float32).astype(ml_dtypes.bfloat16)
        out.append(piece)
        rest = rest - piece.astype(np.float64)
    return np.stack(out)


def _ext_cells():
    cells = [(w, y) for w in range(BZ) for y in range(BY)]
    cells += [(w, y) for w in range(BZ) for y in range(-3, 0)]
    cells += [(w, y) for w in range(BZ) for y in range(BY, BY + 3)]
    cells += [(w, y) for w in range(-3, 0) for y in range(BY)]
    cells += [(w, y) for w in range(BZ, BZ + 3) for y in range(BY)]
    return cells


def _difference_matrices():
    place = {cell: i for i, cell in enumerate(_ext_cells())}
    along_y = np.zeros((CELLS, EXT))
    along_z = np.zeros((CELLS, EXT))
    for w in range(BZ):
        for y in range(BY):
            row = place[(w, y)]
            for k, c in COEF.items():
                along_y[row, place[(w, y + k)]] = c
                along_z[row, place[(w + k, y)]] = c
    return along_y, along_z


def _circulant_x():
    table = np.zeros((NX, NX))
    for x in range(NX):
        for k, c in COEF.items():
            table[(x + k) % NX, x] = c
    return table


def _kt(modes, length):
    a = 2.0 * np.pi * modes / length
    return 1.5 * np.sin(a) - 0.3 * np.sin(2 * a) + np.sin(3 * a) / 30.0


def _x_tables():
    k = np.arange(NX // 2)[:, None]
    x = np.arange(NX)[None, :]
    angle = 2.0 * np.pi * ((k * x) % NX) / NX
    alternating = 1.0 - 2.0 * (np.arange(NX) % 2)
    forward = np.zeros((NX // 2, 2, NX))
    forward[:, 0], forward[:, 1] = np.cos(angle), -np.sin(angle)
    forward[0, 0], forward[0, 1] = 1.0, alternating
    inverse = 2.0 * forward
    inverse[0] = forward[0]
    symbol = _kt(k, NX)
    slope = np.zeros((NX // 2, 2, NX))
    slope[:, 0], slope[:, 1] = -2.0 * symbol * np.sin(angle), -2.0 * symbol * np.cos(angle)
    slope[0] = 0.0
    order = np.arange(NX).reshape(DEV, 4).T.reshape(-1)
    return (
        forward.reshape(NX, NX) / 60.0,
        inverse.reshape(NX, NX)[order] / 60.0,
        slope.reshape(NX, NX)[order],
    )


def _plane_tables():
    a = np.arange(DEV)
    m1, n1 = a // GZ, a % GZ
    gy, gz = a // GZ, a % GZ
    outer = np.exp(
        -2j * np.pi * (np.outer(m1, gy) / GY + np.outer(n1, gz) / GZ)
    )
    cells = np.array(_ext_cells())
    count = len(cells)
    w, y = cells[:, 0], cells[:, 1]
    twist = np.zeros((DEV, EXT), complex)
    twist[:, :count] = np.exp(-2j * np.pi * (np.outer(n1, w) / NZ + np.outer(m1, y) / NY))
    b = np.arange(CELLS)
    n2, m2 = b // BY, b % BY
    inner = np.zeros((EXT, CELLS), complex)
    inner[:count] = np.exp(-2j * np.pi * (np.outer(w, n2) / BZ + np.outer(y, m2) / BY))
    outer_real = np.block([[outer.real, -outer.imag], [outer.imag, outer.real]])
    inner_real = np.block([[inner.real, inner.imag], [-inner.imag, inner.real]])
    mode_y = m1[:, None] + GY * m2[None, :]
    mode_z = n1[:, None] + GZ * n2[None, :]
    edge = (((2 * mode_y) % NY == 0) & ((2 * mode_z) % NZ == 0)).astype(np.float32)
    waves = np.stack([_kt(mode_y, NY), _kt(mode_z, NZ), edge]).astype(np.float32)
    return outer_real, np.stack([twist.real, twist.imag]).astype(np.float32), inner_real, waves


def _exact(table):
    return np.asarray(table, np.float32).astype(ml_dtypes.bfloat16)


def _dot(left, right):
    return lax.dot_general(left, right, (((1,), (0,)), ((), ())), preferred_element_type=F32)


def _dot_nt(left, right):
    return lax.dot_general(left, right, (((1,), (1,)), ((), ())), preferred_element_type=F32)


def _split(value, count):
    out = []
    for i in range(count):
        piece = value.astype(BF16)
        out.append(piece)
        if i + 1 < count:
            value = value - piece.astype(F32)
    return out


PAIRS_3 = ((0, 0), (0, 1), (1, 0))
PAIRS_6 = ((0, 0), (0, 1), (1, 0), (1, 1), (0, 2), (2, 0))


def _passes(left, right, pairs, dot=_dot):
    total = None
    for i, j in reversed(pairs):
        term = dot(left[i], right[j])
        total = term if total is None else total + term
    return total


VMEM = pl.BlockSpec(memory_space=pltpu.VMEM)
SMEM = pl.BlockSpec(memory_space=pltpu.SMEM)


def _call(kernel, out_shape, in_specs, name, flops, nbytes, vmem):
    return pl.pallas_call(
        kernel,
        out_shape=out_shape,
        in_specs=in_specs,
        out_specs=jax.tree.map(lambda _: VMEM, out_shape),
        compiler_params=pltpu.CompilerParams(vmem_limit_bytes=vmem * MIB),
        cost_estimate=pl.CostEstimate(flops=flops, bytes_accessed=nbytes, transcendentals=0),
        name=name,
    )


def edges_kernel(state, pick, y_low, y_high, z_low, z_high):
    for q in range(4):
        rows = _dot(pick[...], state[q])
        y_low[q] = rows[0:96].astype(BF16)
        y_high[q] = rows[96:192].astype(BF16)
        z_low[q] = rows[192:216].astype(BF16)
        z_high[q] = rows[216:240].astype(BF16)


def local_kernel(metric, strain, state, z_below, z_above, along_x, along_y, partial, carrier):
    speeds = [state[q].astype(F32) for q in range(4)]
    contra = [
        metric[0, j] * speeds[0] + metric[1, j] * speeds[1] + metric[2, j] * speeds[2]
        for j in range(3)
    ]
    scale = -STEP / 60.0
    carrier[...] = scale * contra[1]
    for q in range(4):
        d_x = _dot(state[q], along_x[...])
        d_y = _dot(along_y[...], state[q])
        tall = jnp.concatenate(
            [z_below[q].astype(F32), speeds[q], z_above[q].astype(F32)], axis=0
        )

        def moved(k):
            return tall[(3 + k) * BY : (3 + k) * BY + CELLS]

        d_z = (
            45.0 * (moved(1) - moved(-1)) - 9.0 * (moved(2) - moved(-2)) + (moved(3) - moved(-3))
        )
        carried = contra[0] * d_x + contra[1] * d_y + contra[2] * d_z
        if q < 3:
            rest = strain[q, 0] * speeds[0] + strain[q, 1] * speeds[1] + strain[q, 2] * speeds[2]
            if q == 2:
                rest = rest - speeds[3]
        else:
            rest = speeds[2]
        partial[q] = speeds[q] + scale * carried - STEP * rest


def forward_kernel(
    metric, partial, carrier, y_below, y_above, along_y, spread, along_x, waves, provisional, heat, sent
):
    def complete(q):
        beside = jnp.concatenate([y_below[q], y_above[q]], axis=0)
        return partial[q] + carrier[...] * _dot(along_y[...], beside)

    heat[...] = complete(3)
    fields = [complete(q) for q in range(3)]
    for q in range(3):
        provisional[q] = fields[q]
    flux = [
        metric[0, j] * fields[0] + metric[1, j] * fields[1] + metric[2, j] * fields[2]
        for j in range(3)
    ]
    flux = [_split(f, 2) for f in flux]
    lows = jnp.concatenate([flux[1][1], flux[2][1]], axis=0)
    highs = jnp.concatenate([flux[1][0], flux[2][0]], axis=0)
    extended = _dot(spread[...], lows) + _dot(spread[...], highs)
    own = _dot(flux[0][1], along_x[...]) + _dot(flux[0][0], along_x[...])
    extended = jnp.concatenate([extended[:CELLS] + own, extended[CELLS:]], axis=0)
    pieces = _split(extended, 2)
    spectrum = _passes([waves[0], waves[1]], pieces, PAIRS_3, _dot_nt)
    for t in range(EXT // 128):
        sent[:, 4 * t : 4 * t + 4, :] = spectrum[:, 128 * t : 128 * t + 128].reshape(DEV, 4, 128)


def plane_kernel(
    metric, wave_x, got, outer, outer_back, twist, inner, inner_back, waves, sent
):
    here = lax.axis_index("gy") * GZ + lax.axis_index("gz")

    def received(c, part):
        return jnp.concatenate(
            [got[:, 4 * t + 2 * c + part, :] for t in range(EXT // 128)], axis=1
        )

    tr, ti = twist[0], twist[1]
    rows = []
    for c in range(2):
        block = jnp.concatenate([received(c, 0), received(c, 1)], axis=0)
        block = _passes([outer[0], outer[1]], _split(block, 2), PAIRS_3)
        re, im = block[:DEV], block[DEV:]
        rows.append(jnp.concatenate([re * tr - im * ti, re * ti + im * tr], axis=1))
    modes = _passes(
        _split(jnp.concatenate(rows, axis=0), 2), [inner[0], inner[1]], PAIRS_3
    )
    wave_y, wave_z, edge = waves[0], waves[1], waves[2]
    solved = []
    for c in range(2):
        wx = wave_x[2 * here + c]
        symbol = jnp.zeros((DEV, CELLS), F32)
        for i in range(3):
            mixed = metric[i, 0] * wx + metric[i, 1] * wave_y + metric[i, 2] * wave_z
            symbol = symbol + mixed * mixed
        out = (edge * jnp.where(2 * here + c == 0, 1.0, 0.0)) > 0.5
        factor = jnp.where(out, 0.0, -1.0 / (jnp.where(out, 1.0, symbol) * float(NX * NY * NZ)))
        block = modes[c * DEV : (c + 1) * DEV]
        solved.append(block * jnp.concatenate([factor, factor], axis=1))
    cells = _passes(
        _split(jnp.concatenate(solved, axis=0), 3),
        [inner_back[0], inner_back[1], inner_back[2]],
        PAIRS_6,
    )
    for c in range(2):
        re = cells[c * DEV : (c + 1) * DEV, :EXT]
        im = cells[c * DEV : (c + 1) * DEV, EXT:]
        block = jnp.concatenate([re * tr + im * ti, im * tr - re * ti], axis=0)
        block = _passes(
            [outer_back[0], outer_back[1], outer_back[2]], _split(block, 3), PAIRS_6
        )
        for part in range(2):
            for t in range(EXT // 128):
                sent[:, 4 * t + 2 * c + part, :] = block[
                    part * DEV : (part + 1) * DEV, 128 * t : 128 * t + 128
                ]


def project_kernel(metric, got, gather, inverse, slope, provisional, motion):
    rows = [
        jnp.concatenate([got[:, 4 * t + r, :] for t in range(EXT // 128)], axis=1)
        for r in range(4)
    ]
    pieces = _split(jnp.concatenate(rows, axis=0), 3)
    fields = None
    for piece in reversed(pieces):
        term = _dot_nt(gather[...], piece)
        fields = term if fields is None else fields + term
    pushes = []
    for j, table in enumerate((slope, inverse, inverse)):
        left = _split(fields[j * CELLS : (j + 1) * CELLS], 2)
        pushes.append(_passes(left, [table[0], table[1]], PAIRS_3))
    for i in range(3):
        motion[i] = provisional[i] - (
            metric[i, 0] * pushes[0] + metric[i, 1] * pushes[1] + metric[i, 2] * pushes[2]
        )


def _ring(count, shift):
    return [(i, (i + shift) % count) for i in range(count)]


def _step(state, metric, strain):
    along_y, along_z = _difference_matrices()
    forward, inverse, slope = _x_tables()
    outer, twist, inner, waves = _plane_tables()
    k = np.arange(NX // 2)
    wave_x = _kt(k, NX).astype(np.float32)
    wave_x[0] = 0.0
    pick = np.zeros((240, CELLS))
    own = [(w, y) for w in range(BZ) for y in range(BY)]
    place = {cell: i for i, cell in enumerate(own)}
    chosen = [(w, y) for w in range(BZ) for y in range(3)]
    chosen += [(w, y) for w in range(BZ) for y in range(BY - 3, BY)]
    chosen += [(w, y) for w in range(3) for y in range(BY)]
    chosen += [(w, y) for w in range(BZ - 3, BZ) for y in range(BY)]
    for i, cell in enumerate(chosen):
        pick[i, place[cell]] = 1.0
    circulant = _exact(_circulant_x())
    spread = _exact(-np.concatenate([along_y, along_z], axis=0).T)
    gather = _exact(np.concatenate([np.eye(CELLS, EXT), along_y, along_z], axis=0))

    field = jax.ShapeDtypeStruct((CELLS, NX), F32)
    fields = lambda count: jax.ShapeDtypeStruct((count, CELLS, NX), F32)
    block = jax.ShapeDtypeStruct((DEV, 16, 128), F32)
    state = state.reshape(4, CELLS, NX)

    y_side = jax.ShapeDtypeStruct((4, 96, NX), BF16)
    z_side = jax.ShapeDtypeStruct((4, 24, NX), BF16)
    y_low, y_high, z_low, z_high = _call(
        edges_kernel, (y_side, y_side, z_side, z_side), [VMEM, VMEM], "edges", 250_000_000, 2 * MIB, 16
    )(state, _exact(pick))
    y_below = lax.ppermute(y_high, "gy", _ring(GY, 1))
    y_above = lax.ppermute(y_low, "gy", _ring(GY, -1))
    z_below = lax.ppermute(z_high, "gz", _ring(GZ, 1))
    z_above = lax.ppermute(z_low, "gz", _ring(GZ, -1))

    partial, carrier = _call(
        local_kernel, (fields(4), field), [SMEM, SMEM] + [VMEM] * 5, "local", 1_000_000_000, 4 * MIB, 32
    )(metric, strain, state, z_below, z_above, circulant, _exact(along_y[:, :CELLS]))

    provisional, heat, sent = _call(
        forward_kernel,
        (fields(3), field, block),
        [SMEM] + [VMEM] * 8,
        "forward",
        2_000_000_000,
        8 * MIB,
        40,
    )(
        metric,
        partial,
        carrier,
        y_below,
        y_above,
        _exact(along_y[:, CELLS : CELLS + 192]),
        spread,
        circulant,
        _pieces(forward, 2),
    )
    got = lax.all_to_all(sent, ("gy", "gz"), split_axis=0, concat_axis=0, tiled=True)
    sent = _call(
        plane_kernel, block, [SMEM, SMEM] + [VMEM] * 7, "plane", 3_600_000_000, 8 * MIB, 48
    )(
        metric,
        wave_x,
        got,
        _pieces(outer, 2),
        _pieces(outer.T, 3),
        twist,
        _pieces(inner, 2),
        _pieces(inner.T, 3),
        waves,
    )
    got = lax.all_to_all(sent, ("gy", "gz"), split_axis=0, concat_axis=0, tiled=True)
    motion = _call(
        project_kernel, fields(3), [SMEM] + [VMEM] * 5, "project", 2_500_000_000, 8 * MIB, 40
    )(metric, got, gather, _pieces(inverse, 2), _pieces(slope, 2), provisional)
    return motion.reshape(3, BZ, BY, NX), heat.reshape(BZ, BY, NX)


def solution(mesh):
    return jax.shard_map(
        _step,
        mesh=mesh,
        in_specs=(P(None, "gz", "gy", None), P(), P()),
        out_specs=(P(None, "gz", "gy", None), P("gz", "gy", None)),
        check_vma=False,
    )
```

```python
import numpy as np

import jax
import jax.numpy as jnp
import ml_dtypes
from jax import lax
from jax.experimental import pallas as pl
from jax.experimental.pallas import tpu as pltpu
from jax.sharding import PartitionSpec as P

F32 = jnp.float32
BF16 = jnp.bfloat16
NX, NY, NZ = 512, 256, 128
GY, GZ = 32, 4
BY, BZ = NY // GY, NZ // GZ
DEV = GY * GZ
CELLS = BY * BZ
EXT = 512
STEP = 0.4
COEF = {1: 45.0, -1: -45.0, 2: -9.0, -2: 9.0, 3: 1.0, -3: -1.0}
MIB = 1 << 20


def _pieces(table, count):
    rest = np.asarray(table, np.float64)
    out = []
    for _ in range(count):
        piece = rest.astype(np.float32).astype(ml_dtypes.bfloat16)
        out.append(piece)
        rest = rest - piece.astype(np.float64)
    return np.stack(out)


def _ext_cells():
    cells = [(w, y) for w in range(BZ) for y in range(BY)]
    cells += [(w, y) for w in range(BZ) for y in range(-3, 0)]
    cells += [(w, y) for w in range(BZ) for y in range(BY, BY + 3)]
    cells += [(w, y) for w in range(-3, 0) for y in range(BY)]
    cells += [(w, y) for w in range(BZ, BZ + 3) for y in range(BY)]
    return cells


def _difference_matrices():
    place = {cell: i for i, cell in enumerate(_ext_cells())}
    along_y = np.zeros((CELLS, EXT))
    along_z = np.zeros((CELLS, EXT))
    for w in range(BZ):
        for y in range(BY):
            row = place[(w, y)]
            for k, c in COEF.items():
                along_y[row, place[(w, y + k)]] = c
                along_z[row, place[(w + k, y)]] = c
    return along_y, along_z


def _circulant_x():
    table = np.zeros((NX, NX))
    for x in range(NX):
        for k, c in COEF.items():
            table[(x + k) % NX, x] = c
    return table


def _kt(modes, length):
    a = 2.0 * np.pi * modes / length
    return 1.5 * np.sin(a) - 0.3 * np.sin(2 * a) + np.sin(3 * a) / 30.0


def _x_tables():
    k = np.arange(NX // 2)[:, None]
    x = np.arange(NX)[None, :]
    angle = 2.0 * np.pi * ((k * x) % NX) / NX
    alternating = 1.0 - 2.0 * (np.arange(NX) % 2)
    forward = np.zeros((NX // 2, 2, NX))
    forward[:, 0], forward[:, 1] = np.cos(angle), -np.sin(angle)
    forward[0, 0], forward[0, 1] = 1.0, alternating
    inverse = 2.0 * forward
    inverse[0] = forward[0]
    symbol = _kt(k, NX)
    slope = np.zeros((NX // 2, 2, NX))
    slope[:, 0], slope[:, 1] = -2.0 * symbol * np.sin(angle), -2.0 * symbol * np.cos(angle)
    slope[0] = 0.0
    order = np.arange(NX).reshape(DEV, 4).T.reshape(-1)
    return (
        forward.reshape(NX, NX) / 60.0,
        inverse.reshape(NX, NX)[order] / 60.0,
        slope.reshape(NX, NX)[order],
    )


def _plane_tables():
    a = np.arange(DEV)
    m1, n1 = a // GZ, a % GZ
    gy, gz = a // GZ, a % GZ
    outer = np.exp(
        -2j * np.pi * (np.outer(m1, gy) / GY + np.outer(n1, gz) / GZ)
    )
    cells = np.array(_ext_cells())
    count = len(cells)
    w, y = cells[:, 0], cells[:, 1]
    twist = np.zeros((DEV, EXT), complex)
    twist[:, :count] = np.exp(-2j * np.pi * (np.outer(n1, w) / NZ + np.outer(m1, y) / NY))
    b = np.arange(CELLS)
    n2, m2 = b // BY, b % BY
    inner = np.zeros((EXT, CELLS), complex)
    inner[:count] = np.exp(-2j * np.pi * (np.outer(w, n2) / BZ + np.outer(y, m2) / BY))
    outer_real = np.block([[outer.real, -outer.imag], [outer.imag, outer.real]])
    inner_real = np.block([[inner.real, inner.imag], [-inner.imag, inner.real]])
    mode_y = m1[:, None] + GY * m2[None, :]
    mode_z = n1[:, None] + GZ * n2[None, :]
    edge = (((2 * mode_y) % NY == 0) & ((2 * mode_z) % NZ == 0)).astype(np.float32)
    waves = np.stack([_kt(mode_y, NY), _kt(mode_z, NZ), edge]).astype(np.float32)
    return outer_real, np.stack([twist.real, twist.imag]).astype(np.float32), inner_real, waves


def _exact(table):
    return np.asarray(table, np.float32).astype(ml_dtypes.bfloat16)


def _dot(left, right):
    return lax.dot_general(left, right, (((1,), (0,)), ((), ())), preferred_element_type=F32)


def _dot_nt(left, right):
    return lax.dot_general(left, right, (((1,), (1,)), ((), ())), preferred_element_type=F32)


def _split(value, count):
    out = []
    for i in range(count):
        piece = value.astype(BF16)
        out.append(piece)
        if i + 1 < count:
            value = value - piece.astype(F32)
    return out


def _by_table(pieces, table, depth):
    total = None
    for i in reversed(range(len(pieces))):
        count = len(pieces) - i
        left = jnp.concatenate([pieces[i]] * count, axis=1) if count > 1 else pieces[i]
        term = _dot(left, table[: depth * count])
        total = term if total is None else total + term
    return total


def _table_by(table, pieces, depth):
    total = None
    for i in reversed(range(len(pieces))):
        count = len(pieces) - i
        right = jnp.concatenate([pieces[i]] * count, axis=0) if count > 1 else pieces[i]
        term = _dot(table[:, : depth * count], right)
        total = term if total is None else total + term
    return total


VMEM = pl.BlockSpec(memory_space=pltpu.VMEM)
SMEM = pl.BlockSpec(memory_space=pltpu.SMEM)
ANY = pl.BlockSpec(memory_space=pl.ANY)


def _call(kernel, out_shape, in_specs, name, flops, nbytes, vmem, scratch_shapes=(), out_specs=None):
    return pl.pallas_call(
        kernel,
        out_shape=out_shape,
        in_specs=in_specs,
        out_specs=out_specs or jax.tree.map(lambda _: VMEM, out_shape),
        scratch_shapes=scratch_shapes,
        compiler_params=pltpu.CompilerParams(vmem_limit_bytes=vmem * MIB),
        cost_estimate=pl.CostEstimate(flops=flops, bytes_accessed=nbytes, transcendentals=0),
        name=name,
    )


def _picked(state):
    row = lax.broadcasted_iota(jnp.int32, (240, CELLS), 0)
    column = lax.broadcasted_iota(jnp.int32, (240, CELLS), 1)
    high = row >= 96
    within = jnp.where(high, row - 96, row)
    third = (within * 171) >> 9
    along_y = BY * third + (within - 3 * third) + jnp.where(high, BY - 3, 0)
    along_z = jnp.where(row >= 216, row - 216 + CELLS - 24, row - 192)
    source = jnp.where(row >= 192, along_z, along_y)
    pick = jnp.where(column == source, 1.0, 0.0).astype(BF16)
    return [_dot(pick, value) for value in state]


def _store_sides(q, rows, y_low, y_high, z_low, z_high):
    y_low[q] = rows[0:96].astype(BF16)
    y_high[q] = rows[96:192].astype(BF16)
    z_low[q] = rows[192:216].astype(BF16)
    z_high[q] = rows[216:240].astype(BF16)


def edges_kernel(state, *sides):
    for q, rows in enumerate(_picked([state[q] for q in range(4)])):
        _store_sides(q, rows, *sides)


def local_kernel(
    metric, strain, state, along, partial, carrier_y, carrier_z
):
    along_x, along_y = along[:NX], along[NX:, :CELLS]
    speeds = [state[q].astype(F32) for q in range(4)]
    contra = [
        metric[0, j] * speeds[0] + metric[1, j] * speeds[1] + metric[2, j] * speeds[2]
        for j in range(3)
    ]
    scale = -STEP / 60.0
    carrier_y[...] = scale * contra[1]
    carrier_z[0:24] = scale * contra[2][0:24]
    carrier_z[24:48] = scale * contra[2][CELLS - 24 :]
    nothing = jnp.zeros((24, NX), F32)
    for q in range(4):
        d_x = _dot(state[q], along_x)
        d_y = _dot(along_y, state[q])
        tall = jnp.concatenate([nothing, speeds[q], nothing], axis=0)

        def moved(k):
            return tall[(3 + k) * BY : (3 + k) * BY + CELLS]

        d_z = (
            45.0 * (moved(1) - moved(-1)) - 9.0 * (moved(2) - moved(-2)) + (moved(3) - moved(-3))
        )
        carried = contra[0] * d_x + contra[1] * d_y + contra[2] * d_z
        if q < 3:
            rest = strain[q, 0] * speeds[0] + strain[q, 1] * speeds[1] + strain[q, 2] * speeds[2]
            if q == 2:
                rest = rest - speeds[3]
        else:
            rest = speeds[2]
        partial[q] = speeds[q] + scale * carried - STEP * rest


def _complete(q, partial, carrier_y, carrier_z, y_below, y_above, z_below, z_above, along_y, along_z):
    beside = jnp.concatenate([y_below[q], y_above[q]], axis=0)
    whole = partial + carrier_y[...] * _dot(along_y[...], beside)
    low = whole[:24] + carrier_z[0:24] * _dot(along_z[0], z_below[q])
    high = whole[CELLS - 24 :] + carrier_z[24:48] * _dot(along_z[1], z_above[q])
    return jnp.concatenate([low, whole[24 : CELLS - 24], high], axis=0)


def forward_kernel(
    metric,
    partial,
    carrier_y,
    carrier_z,
    y_below,
    y_above,
    z_below,
    z_above,
    along_y,
    along_z,
    spread,
    along_x,
    waves,
    provisional,
    sent,
    heat,
    held,
    done,
):
    fields = [
        _complete(
            q, partial[q], carrier_y, carrier_z, y_below, y_above, z_below, z_above, along_y, along_z
        )
        for q in range(4)
    ]
    held[...] = fields[3]
    copy = pltpu.make_async_copy(held, heat, done)
    copy.start()
    for q in range(3):
        provisional[q] = fields[q]
    flux = [
        metric[0, j] * fields[0] + metric[1, j] * fields[1] + metric[2, j] * fields[2]
        for j in range(3)
    ]
    flux = [_split(f, 2) for f in flux]
    stacked = jnp.concatenate([flux[1][0], flux[2][0], flux[1][1], flux[2][1]], axis=0)
    extended = _dot(spread[...], stacked)
    own = _dot(jnp.concatenate(flux[0], axis=1), along_x[...])
    extended = jnp.concatenate([extended[:CELLS] + own, extended[CELLS:]], axis=0)
    high, low = _split(extended, 2)
    spectrum = _dot_nt(waves[:, :NX], low) + _dot_nt(
        waves[...], jnp.concatenate([high, high], axis=1)
    )
    for t in range(EXT // 128):
        sent[:, 4 * t : 4 * t + 4, :] = spectrum[:, 128 * t : 128 * t + 128].reshape(DEV, 4, 128)
    copy.wait()


def plane_kernel(
    metric,
    wave_x,
    got,
    outer,
    outer_back,
    twist,
    inner,
    inner_back,
    waves,
    sent,
):
    here = lax.axis_index("gy") * GZ + lax.axis_index("gz")

    def received(part):
        return jnp.concatenate(
            [got[:, 4 * t + 2 * c + part, :] for c in range(2) for t in range(EXT // 128)], axis=1
        )

    tr, ti = twist[0], twist[1]
    block = jnp.concatenate([received(0), received(1)], axis=0)
    block = _table_by(outer, _split(block, 2), 2 * DEV)
    rows = []
    for c in range(2):
        re, im = block[:DEV, c * EXT : (c + 1) * EXT], block[DEV:, c * EXT : (c + 1) * EXT]
        rows.append(jnp.concatenate([re * tr - im * ti, re * ti + im * tr], axis=1))
    modes = _by_table(_split(jnp.concatenate(rows, axis=0), 2), inner, 2 * EXT)
    wave_y, wave_z, edge = waves[0], waves[1], waves[2]
    solved = []
    for c in range(2):
        wx = wave_x[2 * here + c]
        symbol = jnp.zeros((DEV, CELLS), F32)
        for i in range(3):
            mixed = metric[i, 0] * wx + metric[i, 1] * wave_y + metric[i, 2] * wave_z
            symbol = symbol + mixed * mixed
        out = (edge * jnp.where(2 * here + c == 0, 1.0, 0.0)) > 0.5
        factor = jnp.where(out, 0.0, -1.0 / (jnp.where(out, 1.0, symbol) * float(NX * NY * NZ)))
        block = modes[c * DEV : (c + 1) * DEV]
        solved.append(block * jnp.concatenate([factor, factor], axis=1))
    cells = _by_table(_split(jnp.concatenate(solved, axis=0), 3), inner_back, 2 * CELLS)
    columns = []
    for c in range(2):
        re = cells[c * DEV : (c + 1) * DEV, :EXT]
        im = cells[c * DEV : (c + 1) * DEV, EXT:]
        columns.append(jnp.concatenate([re * tr + im * ti, im * tr - re * ti], axis=0))
    block = _table_by(outer_back, _split(jnp.concatenate(columns, axis=1), 3), 2 * DEV)
    for c in range(2):
        for part in range(2):
            for t in range(EXT // 128):
                at = c * EXT + 128 * t
                sent[:, 4 * t + 2 * c + part, :] = block[part * DEV : (part + 1) * DEV, at : at + 128]


def project_kernel(metric, got, gather, inverse, slope, provisional, motion):
    rows = [
        jnp.concatenate([got[:, 4 * t + r, :] for t in range(EXT // 128)], axis=1)
        for r in range(4)
    ]
    pieces = jnp.concatenate(_split(jnp.concatenate(rows, axis=0), 3), axis=1)
    fields = _dot_nt(gather[...], pieces)
    pushes = []
    for j, table in enumerate((slope, inverse, inverse)):
        left = _split(fields[j * CELLS : (j + 1) * CELLS], 2)
        pushes.append(_by_table(left, table, NX))
    for i in range(3):
        motion[i] = provisional[i] - (
            metric[i, 0] * pushes[0] + metric[i, 1] * pushes[1] + metric[i, 2] * pushes[2]
        )


def _ring(count, shift):
    return [(i, (i + shift) % count) for i in range(count)]


def _step(state, metric, strain):
    along_y, along_z = _difference_matrices()
    forward, inverse, slope = _x_tables()
    outer, twist, inner, waves = _plane_tables()
    k = np.arange(NX // 2)
    wave_x = _kt(k, NX).astype(np.float32)
    wave_x[0] = 0.0
    circulant = _exact(_circulant_x())
    spread = _exact(-np.concatenate([along_y, along_z], axis=0).T)
    spread = np.concatenate([spread, spread], axis=1)
    gather = _exact(np.concatenate([np.eye(CELLS, EXT), along_y, along_z], axis=0))
    gather = np.concatenate([gather] * 3, axis=1)
    beside_y = _exact(along_y[:, CELLS : CELLS + 192])
    beside_z = _exact(
        np.stack([along_z[:24, CELLS + 192 : CELLS + 216], along_z[CELLS - 24 :, CELLS + 216 : CELLS + 240]])
    )
    local = np.zeros((NX + CELLS, NX))
    local[:NX] = _circulant_x()
    local[NX:, :CELLS] = along_y[:, :CELLS]

    field = jax.ShapeDtypeStruct((CELLS, NX), F32)
    fields = lambda count: jax.ShapeDtypeStruct((count, CELLS, NX), F32)
    block = jax.ShapeDtypeStruct((DEV, 16, 128), F32)
    state = state.reshape(4, CELLS, NX)

    def sides(count):
        y_side = jax.ShapeDtypeStruct((count, 96, NX), BF16)
        z_side = jax.ShapeDtypeStruct((count, 24, NX), BF16)
        return (y_side, y_side, z_side, z_side)

    def exchange(y_low, y_high, z_low, z_high):
        return (
            lax.ppermute(y_high, "gy", _ring(GY, 1)),
            lax.ppermute(y_low, "gy", _ring(GY, -1)),
            lax.ppermute(z_high, "gz", _ring(GZ, 1)),
            lax.ppermute(z_low, "gz", _ring(GZ, -1)),
        )

    beside = exchange(*_call(edges_kernel, sides(4), [VMEM], "edges", 200_000_000, 2 * MIB, 16)(state))
    partial, carrier_y, carrier_z = _call(
        local_kernel,
        (fields(4), field, jax.ShapeDtypeStruct((48, NX), F32)),
        [SMEM, SMEM, VMEM, VMEM],
        "local",
        1_000_000_000,
        4 * MIB,
        24,
    )(metric, strain, state, _exact(local))

    provisional, sent, heat = _call(
        forward_kernel,
        (fields(3), block, field),
        [SMEM] + [VMEM] * 12,
        "forward",
        2_000_000_000,
        8 * MIB,
        40,
        out_specs=(VMEM, VMEM, ANY),
        scratch_shapes=[pltpu.VMEM((CELLS, NX), F32), pltpu.SemaphoreType.DMA],
    )(
        metric,
        partial,
        carrier_y,
        carrier_z,
        *beside,
        beside_y,
        beside_z,
        spread,
        np.concatenate([circulant, circulant], axis=0),
        np.concatenate(_pieces(forward, 2), axis=1),
    )
    got = lax.all_to_all(sent, ("gy", "gz"), split_axis=0, concat_axis=0, tiled=True)
    sent = _call(
        plane_kernel, block, [SMEM, SMEM] + [VMEM] * 7, "plane", 3_600_000_000, 8 * MIB, 40
    )(
        metric,
        wave_x,
        got,
        np.concatenate(_pieces(outer, 2), axis=1),
        np.concatenate(_pieces(outer.T, 3), axis=1),
        twist,
        np.concatenate(_pieces(inner, 2), axis=0),
        np.concatenate(_pieces(inner.T, 3), axis=0),
        waves,
    )
    got = lax.all_to_all(sent, ("gy", "gz"), split_axis=0, concat_axis=0, tiled=True)
    motion = _call(
        project_kernel, fields(3), [SMEM] + [VMEM] * 5, "project", 2_500_000_000, 8 * MIB, 40
    )(
        metric,
        got,
        gather,
        np.concatenate(_pieces(inverse, 2), axis=0),
        np.concatenate(_pieces(slope, 2), axis=0),
        provisional,
    )
    return motion.reshape(3, BZ, BY, NX), heat.reshape(BZ, BY, NX)


def solution(mesh):
    return jax.shard_map(
        _step,
        mesh=mesh,
        in_specs=(P(None, "gz", "gy", None), P(), P()),
        out_specs=(P(None, "gz", "gy", None), P("gz", "gy", None)),
        check_vma=False,
    )
```

```python
import numpy as np

import jax
import jax.numpy as jnp
import ml_dtypes
from jax import lax
from jax.experimental import pallas as pl
from jax.experimental.pallas import tpu as pltpu
from jax.sharding import PartitionSpec as P

F32 = jnp.float32
BF16 = jnp.bfloat16
NX, NY, NZ = 512, 256, 128
GY, GZ = 32, 4
BY, BZ = NY // GY, NZ // GZ
DEV = GY * GZ
CELLS = BY * BZ
EXT = 512
STEP = 0.4
COEF = {1: 45.0, -1: -45.0, 2: -9.0, -2: 9.0, 3: 1.0, -3: -1.0}
MIB = 1 << 20


def _pieces(table, count):
    rest = np.asarray(table, np.float64)
    out = []
    for _ in range(count):
        piece = rest.astype(np.float32).astype(ml_dtypes.bfloat16)
        out.append(piece)
        rest = rest - piece.astype(np.float64)
    return np.stack(out)


def _ext_cells():
    cells = [(w, y) for w in range(BZ) for y in range(BY)]
    cells += [(w, y) for w in range(BZ) for y in range(-3, 0)]
    cells += [(w, y) for w in range(BZ) for y in range(BY, BY + 3)]
    cells += [(w, y) for w in range(-3, 0) for y in range(BY)]
    cells += [(w, y) for w in range(BZ, BZ + 3) for y in range(BY)]
    return cells


def _difference_matrices():
    place = {cell: i for i, cell in enumerate(_ext_cells())}
    along_y = np.zeros((CELLS, EXT))
    along_z = np.zeros((CELLS, EXT))
    for w in range(BZ):
        for y in range(BY):
            row = place[(w, y)]
            for k, c in COEF.items():
                along_y[row, place[(w, y + k)]] = c
                along_z[row, place[(w + k, y)]] = c
    return along_y, along_z


def _circulant_x():
    table = np.zeros((NX, NX))
    for x in range(NX):
        for k, c in COEF.items():
            table[(x + k) % NX, x] = c
    return table


def _kt(modes, length):
    a = 2.0 * np.pi * modes / length
    return 1.5 * np.sin(a) - 0.3 * np.sin(2 * a) + np.sin(3 * a) / 30.0


def _x_tables():
    k = np.arange(NX // 2)[:, None]
    x = np.arange(NX)[None, :]
    angle = 2.0 * np.pi * ((k * x) % NX) / NX
    alternating = 1.0 - 2.0 * (np.arange(NX) % 2)
    forward = np.zeros((NX // 2, 2, NX))
    forward[:, 0], forward[:, 1] = np.cos(angle), -np.sin(angle)
    forward[0, 0], forward[0, 1] = 1.0, alternating
    inverse = 2.0 * forward
    inverse[0] = forward[0]
    symbol = _kt(k, NX)
    slope = np.zeros((NX // 2, 2, NX))
    slope[:, 0], slope[:, 1] = -2.0 * symbol * np.sin(angle), -2.0 * symbol * np.cos(angle)
    slope[0] = 0.0
    order = np.arange(NX).reshape(DEV, 4).T.reshape(-1)
    return (
        forward.reshape(NX, NX) / 60.0,
        inverse.reshape(NX, NX)[order] / 60.0,
        slope.reshape(NX, NX)[order],
    )


def _plane_tables():
    a = np.arange(DEV)
    m1, n1 = a // GZ, a % GZ
    gy, gz = a // GZ, a % GZ
    outer = np.exp(
        -2j * np.pi * (np.outer(m1, gy) / GY + np.outer(n1, gz) / GZ)
    )
    cells = np.array(_ext_cells())
    count = len(cells)
    w, y = cells[:, 0], cells[:, 1]
    twist = np.zeros((DEV, EXT), complex)
    twist[:, :count] = np.exp(-2j * np.pi * (np.outer(n1, w) / NZ + np.outer(m1, y) / NY))
    b = np.arange(CELLS)
    n2, m2 = b // BY, b % BY
    inner = np.zeros((EXT, CELLS), complex)
    inner[:count] = np.exp(-2j * np.pi * (np.outer(w, n2) / BZ + np.outer(y, m2) / BY))
    outer_real = np.block([[outer.real, -outer.imag], [outer.imag, outer.real]])
    inner_real = np.block([[inner.real, inner.imag], [-inner.imag, inner.real]])
    mode_y = m1[:, None] + GY * m2[None, :]
    mode_z = n1[:, None] + GZ * n2[None, :]
    edge = (((2 * mode_y) % NY == 0) & ((2 * mode_z) % NZ == 0)).astype(np.float32)
    waves = np.stack([_kt(mode_y, NY), _kt(mode_z, NZ), edge]).astype(np.float32)
    return outer_real, np.stack([twist.real, twist.imag]).astype(np.float32), inner_real, waves


def _exact(table):
    return np.asarray(table, np.float32).astype(ml_dtypes.bfloat16)


def _dot(left, right):
    return lax.dot_general(left, right, (((1,), (0,)), ((), ())), preferred_element_type=F32)


def _dot_nt(left, right):
    return lax.dot_general(left, right, (((1,), (1,)), ((), ())), preferred_element_type=F32)


def _split(value, count):
    out = []
    for i in range(count):
        piece = value.astype(BF16)
        out.append(piece)
        if i + 1 < count:
            value = value - piece.astype(F32)
    return out


def _by_table(pieces, table, depth):
    total = None
    for i in reversed(range(len(pieces))):
        count = len(pieces) - i
        left = jnp.concatenate([pieces[i]] * count, axis=1) if count > 1 else pieces[i]
        term = _dot(left, table[: depth * count])
        total = term if total is None else total + term
    return total


def _table_by(table, pieces, depth):
    total = None
    for i in reversed(range(len(pieces))):
        count = len(pieces) - i
        right = jnp.concatenate([pieces[i]] * count, axis=0) if count > 1 else pieces[i]
        term = _dot(table[:, : depth * count], right)
        total = term if total is None else total + term
    return total


VMEM = pl.BlockSpec(memory_space=pltpu.VMEM)
SMEM = pl.BlockSpec(memory_space=pltpu.SMEM)
ANY = pl.BlockSpec(memory_space=pl.ANY)


def _call(kernel, out_shape, in_specs, name, flops, nbytes, vmem, scratch_shapes=(), out_specs=None):
    return pl.pallas_call(
        kernel,
        out_shape=out_shape,
        in_specs=in_specs,
        out_specs=out_specs or jax.tree.map(lambda _: VMEM, out_shape),
        scratch_shapes=scratch_shapes,
        compiler_params=pltpu.CompilerParams(vmem_limit_bytes=vmem * MIB),
        cost_estimate=pl.CostEstimate(flops=flops, bytes_accessed=nbytes, transcendentals=0),
        name=name,
    )


def _odd(axis):
    return lax.rem(lax.axis_index(axis), 2)


def edges_kernel(state, y_first, y_second, z_first, z_second):
    odd_y, odd_z = _odd("gy"), _odd("gz")
    row = lax.broadcasted_iota(jnp.int32, (240, CELLS), 0)
    column = lax.broadcasted_iota(jnp.int32, (240, CELLS), 1)
    second = row >= 96
    within = jnp.where(second, row - 96, row)
    third = (within * 171) >> 9
    top_y = (BY - 3) * jnp.where(second, odd_y, 1 - odd_y)
    along_y = BY * third + (within - 3 * third) + top_y
    second = row >= 216
    top_z = (CELLS - 24) * jnp.where(second, odd_z, 1 - odd_z)
    along_z = jnp.where(second, row - 216, row - 192) + top_z
    source = jnp.where(row >= 192, along_z, along_y)
    pick = jnp.where(column == source, 1.0, 0.0).astype(BF16)
    for q in range(4):
        rows = _dot(pick, state[q])
        y_first[q] = rows[0:96].astype(BF16)
        y_second[q] = rows[96:192].astype(BF16)
        z_first[q] = rows[192:216].astype(BF16)
        z_second[q] = rows[216:240].astype(BF16)


def local_kernel(
    metric, strain, state, along, partial, carrier_y, carrier_z
):
    along_x, along_y = along[:NX], along[NX:, :CELLS]
    speeds = [state[q].astype(F32) for q in range(4)]
    contra = [
        metric[0, j] * speeds[0] + metric[1, j] * speeds[1] + metric[2, j] * speeds[2]
        for j in range(3)
    ]
    scale = -STEP / 60.0
    carrier_y[...] = scale * contra[1]
    carrier_z[0:24] = scale * contra[2][0:24]
    carrier_z[24:48] = scale * contra[2][CELLS - 24 :]
    nothing = jnp.zeros((24, NX), F32)
    for q in range(4):
        d_x = _dot(state[q], along_x)
        d_y = _dot(along_y, state[q])
        tall = jnp.concatenate([nothing, speeds[q], nothing], axis=0)

        def moved(k):
            return tall[(3 + k) * BY : (3 + k) * BY + CELLS]

        d_z = (
            45.0 * (moved(1) - moved(-1)) - 9.0 * (moved(2) - moved(-2)) + (moved(3) - moved(-3))
        )
        carried = contra[0] * d_x + contra[1] * d_y + contra[2] * d_z
        if q < 3:
            rest = strain[q, 0] * speeds[0] + strain[q, 1] * speeds[1] + strain[q, 2] * speeds[2]
            if q == 2:
                rest = rest - speeds[3]
        else:
            rest = speeds[2]
        partial[q] = speeds[q] + scale * carried - STEP * rest


def _complete(q, partial, carrier_y, carrier_z, y_first, y_second, z_first, z_second, along_y, along_z):
    odd_y, odd_z = _odd("gy"), _odd("gz")
    beside = jnp.concatenate([y_first[q], y_second[q]], axis=0)
    whole = partial + carrier_y[...] * _dot(along_y[odd_y], beside)
    first, second = _dot(along_z[odd_z], z_first[q]), _dot(along_z[1 - odd_z], z_second[q])
    below = jnp.where(odd_z == 1, first, second)
    above = jnp.where(odd_z == 1, second, first)
    low = whole[:24] + carrier_z[0:24] * below
    high = whole[CELLS - 24 :] + carrier_z[24:48] * above
    return jnp.concatenate([low, whole[24 : CELLS - 24], high], axis=0)


def forward_kernel(
    metric,
    partial,
    carrier_y,
    carrier_z,
    y_first,
    y_second,
    z_first,
    z_second,
    along_y,
    along_z,
    spread,
    along_x,
    waves,
    provisional,
    sent,
    heat,
    held,
    done,
):
    fields = [
        _complete(
            q, partial[q], carrier_y, carrier_z, y_first, y_second, z_first, z_second, along_y, along_z
        )
        for q in range(4)
    ]
    held[...] = fields[3]
    copy = pltpu.make_async_copy(held, heat, done)
    copy.start()
    for q in range(3):
        provisional[q] = fields[q]
    flux = [
        metric[0, j] * fields[0] + metric[1, j] * fields[1] + metric[2, j] * fields[2]
        for j in range(3)
    ]
    flux = [_split(f, 2) for f in flux]
    stacked = jnp.concatenate([flux[1][0], flux[2][0], flux[1][1], flux[2][1]], axis=0)
    extended = _dot(spread[...], stacked)
    own = _dot(jnp.concatenate(flux[0], axis=1), along_x[...])
    extended = jnp.concatenate([extended[:CELLS] + own, extended[CELLS:]], axis=0)
    high, low = _split(extended, 2)
    spectrum = _dot_nt(waves[:, :NX], low) + _dot_nt(
        waves[...], jnp.concatenate([high, high], axis=1)
    )
    for t in range(EXT // 128):
        sent[:, 4 * t : 4 * t + 4, :] = spectrum[:, 128 * t : 128 * t + 128].reshape(DEV, 4, 128)
    copy.wait()


def plane_kernel(
    metric,
    wave_x,
    got,
    outer,
    outer_back,
    twist,
    inner,
    inner_back,
    waves,
    sent,
):
    here = lax.axis_index("gy") * GZ + lax.axis_index("gz")

    def received(part):
        return jnp.concatenate(
            [got[:, 4 * t + 2 * c + part, :] for c in range(2) for t in range(EXT // 128)], axis=1
        )

    tr, ti = twist[0], twist[1]
    block = jnp.concatenate([received(0), received(1)], axis=0)
    block = _table_by(outer, _split(block, 2), 2 * DEV)
    rows = []
    for c in range(2):
        re, im = block[:DEV, c * EXT : (c + 1) * EXT], block[DEV:, c * EXT : (c + 1) * EXT]
        rows.append(jnp.concatenate([re * tr - im * ti, re * ti + im * tr], axis=1))
    modes = _by_table(_split(jnp.concatenate(rows, axis=0), 2), inner, 2 * EXT)
    wave_y, wave_z, edge = waves[0], waves[1], waves[2]
    solved = []
    for c in range(2):
        wx = wave_x[2 * here + c]
        symbol = jnp.zeros((DEV, CELLS), F32)
        for i in range(3):
            mixed = metric[i, 0] * wx + metric[i, 1] * wave_y + metric[i, 2] * wave_z
            symbol = symbol + mixed * mixed
        out = (edge * jnp.where(2 * here + c == 0, 1.0, 0.0)) > 0.5
        factor = jnp.where(out, 0.0, -1.0 / (jnp.where(out, 1.0, symbol) * float(NX * NY * NZ)))
        block = modes[c * DEV : (c + 1) * DEV]
        solved.append(block * jnp.concatenate([factor, factor], axis=1))
    high, low = _split(jnp.concatenate(solved, axis=0), 2)
    cells = _dot(jnp.concatenate([low] * 2, axis=1), inner_back[: 4 * CELLS]) + _dot(
        jnp.concatenate([high] * 3, axis=1), inner_back[...]
    )
    columns = []
    for c in range(2):
        re = cells[c * DEV : (c + 1) * DEV, :EXT]
        im = cells[c * DEV : (c + 1) * DEV, EXT:]
        columns.append(jnp.concatenate([re * tr + im * ti, im * tr - re * ti], axis=0))
    high, middle, low = _split(jnp.concatenate(columns, axis=1), 3)
    block = _dot(outer_back[:, : 2 * DEV], low) + _dot(
        outer_back[...], jnp.concatenate([middle] * 2, axis=0)
    )
    block = block + _dot(outer_back[...], jnp.concatenate([high] * 2, axis=0))
    for c in range(2):
        for part in range(2):
            for t in range(EXT // 128):
                at = c * EXT + 128 * t
                sent[:, 4 * t + 2 * c + part, :] = block[part * DEV : (part + 1) * DEV, at : at + 128]


def project_kernel(metric, got, gather, inverse, slope, provisional, motion, held, done):
    rows = [
        jnp.concatenate([got[:, 4 * t + r, :] for t in range(EXT // 128)], axis=1)
        for r in range(4)
    ]
    pieces = jnp.concatenate(_split(jnp.concatenate(rows, axis=0), 3), axis=1)
    fields = _dot_nt(gather[...], pieces)
    fields = [_split(fields[j * CELLS : (j + 1) * CELLS], 2) for j in range(3)]
    half = NX // 2
    copies = []
    for h in range(2):
        at = pl.ds(h * half, half)
        pushes = [
            _by_table(left, table[:, at], NX)
            for left, table in zip(fields, (slope, inverse, inverse))
        ]
        for i in range(3):
            held[i, :, at] = provisional[i, :, at] - (
                metric[i, 0] * pushes[0] + metric[i, 1] * pushes[1] + metric[i, 2] * pushes[2]
            )
            copy = pltpu.make_async_copy(
                held.at[i, :, at], motion.at[i, :, at], done.at[3 * h + i]
            )
            copy.start()
            copies.append(copy)
    for copy in copies:
        copy.wait()


def _swaps(count):
    first = [(i, i ^ 1) for i in range(count)]
    second = [(i, (i + 1 if i % 2 else i - 1) % count) for i in range(count)]
    return first, second


def _step(state, metric, strain):
    along_y, along_z = _difference_matrices()
    forward, inverse, slope = _x_tables()
    outer, twist, inner, waves = _plane_tables()
    k = np.arange(NX // 2)
    wave_x = _kt(k, NX).astype(np.float32)
    wave_x[0] = 0.0
    circulant = _exact(_circulant_x())
    spread = _exact(-np.concatenate([along_y, along_z], axis=0).T)
    spread = np.concatenate([spread, spread], axis=1)
    gather = _exact(np.concatenate([np.eye(CELLS, EXT), along_y, along_z], axis=0))
    gather = np.concatenate([gather] * 3, axis=1)
    below, above = along_y[:, CELLS : CELLS + 96], along_y[:, CELLS + 96 : CELLS + 192]
    beside_y = _exact(
        np.stack([np.concatenate([above, below], axis=1), np.concatenate([below, above], axis=1)])
    )
    beside_z = _exact(
        np.stack([along_z[CELLS - 24 :, CELLS + 216 : CELLS + 240], along_z[:24, CELLS + 192 : CELLS + 216]])
    )
    local = np.zeros((NX + CELLS, NX))
    local[:NX] = _circulant_x()
    local[NX:, :CELLS] = along_y[:, :CELLS]

    field = jax.ShapeDtypeStruct((CELLS, NX), F32)
    fields = lambda count: jax.ShapeDtypeStruct((count, CELLS, NX), F32)
    block = jax.ShapeDtypeStruct((DEV, 16, 128), F32)
    state = state.reshape(4, CELLS, NX)

    def sides(count):
        y_side = jax.ShapeDtypeStruct((count, 96, NX), BF16)
        z_side = jax.ShapeDtypeStruct((count, 24, NX), BF16)
        return (y_side, y_side, z_side, z_side)

    def exchange(y_first, y_second, z_first, z_second):
        swaps_y, swaps_z = _swaps(GY), _swaps(GZ)
        return (
            lax.ppermute(y_first, "gy", swaps_y[0]),
            lax.ppermute(y_second, "gy", swaps_y[1]),
            lax.ppermute(z_first, "gz", swaps_z[0]),
            lax.ppermute(z_second, "gz", swaps_z[1]),
        )

    beside = exchange(*_call(edges_kernel, sides(4), [VMEM], "edges", 200_000_000, 2 * MIB, 16)(state))
    partial, carrier_y, carrier_z = _call(
        local_kernel,
        (fields(4), field, jax.ShapeDtypeStruct((48, NX), F32)),
        [SMEM, SMEM, VMEM, VMEM],
        "local",
        1_000_000_000,
        4 * MIB,
        24,
    )(metric, strain, state, _exact(local))

    provisional, sent, heat = _call(
        forward_kernel,
        (fields(3), block, field),
        [SMEM] + [VMEM] * 12,
        "forward",
        2_000_000_000,
        8 * MIB,
        40,
        out_specs=(VMEM, VMEM, ANY),
        scratch_shapes=[pltpu.VMEM((CELLS, NX), F32), pltpu.SemaphoreType.DMA],
    )(
        metric,
        partial,
        carrier_y,
        carrier_z,
        *beside,
        beside_y,
        beside_z,
        spread,
        np.concatenate([circulant, circulant], axis=0),
        np.concatenate(_pieces(forward, 2), axis=1),
    )
    got = lax.all_to_all(sent, ("gy", "gz"), split_axis=0, concat_axis=0, tiled=True)
    sent = _call(
        plane_kernel, block, [SMEM, SMEM] + [VMEM] * 7, "plane", 3_600_000_000, 8 * MIB, 40
    )(
        metric,
        wave_x,
        got,
        np.concatenate(_pieces(outer, 2), axis=1),
        np.concatenate(_pieces(outer.T, 2), axis=1),
        twist,
        np.concatenate(_pieces(inner, 2), axis=0),
        np.concatenate(_pieces(inner.T, 3), axis=0),
        waves,
    )
    got = lax.all_to_all(sent, ("gy", "gz"), split_axis=0, concat_axis=0, tiled=True)
    motion = _call(
        project_kernel,
        fields(3),
        [SMEM] + [VMEM] * 5,
        "project",
        2_500_000_000,
        8 * MIB,
        40,
        out_specs=ANY,
        scratch_shapes=[pltpu.VMEM((3, CELLS, NX), F32), pltpu.SemaphoreType.DMA((6,))],
    )(
        metric,
        got,
        gather,
        np.concatenate(_pieces(inverse, 2), axis=0),
        np.concatenate(_pieces(slope, 2), axis=0),
        provisional,
    )
    return motion.reshape(3, BZ, BY, NX), heat.reshape(BZ, BY, NX)


def solution(mesh):
    return jax.shard_map(
        _step,
        mesh=mesh,
        in_specs=(P(None, "gz", "gy", None), P(), P()),
        out_specs=(P(None, "gz", "gy", None), P("gz", "gy", None)),
        check_vma=False,
    )
```

```python
import numpy as np

import jax
import jax.numpy as jnp
import ml_dtypes
from jax import lax
from jax.experimental import pallas as pl
from jax.experimental.pallas import tpu as pltpu
from jax.sharding import PartitionSpec as P

F32 = jnp.float32
BF16 = jnp.bfloat16
NX, NY, NZ = 512, 256, 128
GY, GZ = 32, 4
BY, BZ = NY // GY, NZ // GZ
DEV = GY * GZ
CELLS = BY * BZ
EXT = 512
STEP = 0.4
COEF = {1: 45.0, -1: -45.0, 2: -9.0, -2: 9.0, 3: 1.0, -3: -1.0}
MIB = 1 << 20


def _pieces(table, count):
    rest = np.asarray(table, np.float64)
    out = []
    for _ in range(count):
        piece = rest.astype(np.float32).astype(ml_dtypes.bfloat16)
        out.append(piece)
        rest = rest - piece.astype(np.float64)
    return np.stack(out)


def _ext_cells():
    cells = [(w, y) for w in range(BZ) for y in range(BY)]
    cells += [(w, y) for w in range(BZ) for y in range(-3, 0)]
    cells += [(w, y) for w in range(BZ) for y in range(BY, BY + 3)]
    cells += [(w, y) for w in range(-3, 0) for y in range(BY)]
    cells += [(w, y) for w in range(BZ, BZ + 3) for y in range(BY)]
    return cells


def _difference_matrices():
    place = {cell: i for i, cell in enumerate(_ext_cells())}
    along_y = np.zeros((CELLS, EXT))
    along_z = np.zeros((CELLS, EXT))
    for w in range(BZ):
        for y in range(BY):
            row = place[(w, y)]
            for k, c in COEF.items():
                along_y[row, place[(w, y + k)]] = c
                along_z[row, place[(w + k, y)]] = c
    return along_y, along_z


def _circulant_x():
    table = np.zeros((NX, NX))
    for x in range(NX):
        for k, c in COEF.items():
            table[(x + k) % NX, x] = c
    return table


def _kt(modes, length):
    a = 2.0 * np.pi * modes / length
    return 1.5 * np.sin(a) - 0.3 * np.sin(2 * a) + np.sin(3 * a) / 30.0


def _x_tables():
    k = np.arange(NX // 2)[:, None]
    x = np.arange(NX)[None, :]
    angle = 2.0 * np.pi * ((k * x) % NX) / NX
    alternating = 1.0 - 2.0 * (np.arange(NX) % 2)
    forward = np.zeros((NX // 2, 2, NX))
    forward[:, 0], forward[:, 1] = np.cos(angle), -np.sin(angle)
    forward[0, 0], forward[0, 1] = 1.0, alternating
    inverse = 2.0 * forward
    inverse[0] = forward[0]
    inverse = inverse.reshape(DEV, 2, 2, NX).transpose(1, 2, 0, 3).reshape(2, 2 * DEV, NX)
    symbol = 60.0 * _kt(np.arange(NX // 2), NX)
    symbol[0] = 0.0
    symbol = symbol.reshape(DEV, 2).T.reshape(2, 1, DEV).astype(np.float32)
    inverse = _pieces(inverse / 60.0, 2)
    inverse = np.concatenate(
        [inverse[0, 0], inverse[1, 0], inverse[0, 1], inverse[1, 1], inverse[0, 0], inverse[0, 1]]
    )
    return forward.reshape(NX, NX) / 60.0, inverse, symbol


def _plane_tables():
    a = np.arange(DEV)
    m1, n1 = a // GZ, a % GZ
    gy, gz = a // GZ, a % GZ
    outer = np.exp(
        -2j * np.pi * (np.outer(m1, gy) / GY + np.outer(n1, gz) / GZ)
    )
    cells = np.array(_ext_cells())
    count = len(cells)
    w, y = cells[:, 0], cells[:, 1]
    twist = np.zeros((DEV, EXT), complex)
    twist[:, :count] = np.exp(-2j * np.pi * (np.outer(n1, w) / NZ + np.outer(m1, y) / NY))
    b = np.arange(CELLS)
    n2, m2 = b // BY, b % BY
    inner = np.zeros((EXT, CELLS), complex)
    inner[:count] = np.exp(-2j * np.pi * (np.outer(w, n2) / BZ + np.outer(y, m2) / BY))
    outer_real = np.block([[outer.real, -outer.imag], [outer.imag, outer.real]])
    inner_real = np.block([[inner.real, inner.imag], [-inner.imag, inner.real]])
    chunks = EXT // 128
    inner_back = _pieces(inner_real.T, 3)[[0, 1, 2, 0, 1]].reshape(5, 2 * CELLS, 2, chunks, 128)
    inner_back = inner_back.transpose(0, 1, 3, 2, 4).reshape(10 * CELLS, 1024)
    inner_real = _pieces(inner_real, 2)[[0, 1, 0]].reshape(3, 2, chunks, 128, 2 * CELLS)
    inner_real = inner_real.transpose(2, 0, 1, 3, 4).reshape(chunks * 768, 2 * CELLS)
    mode_y = m1[:, None] + GY * m2[None, :]
    mode_z = n1[:, None] + GZ * n2[None, :]
    edge = (((2 * mode_y) % NY == 0) & ((2 * mode_z) % NZ == 0)).astype(np.float32)
    waves = np.stack([_kt(mode_y, NY), _kt(mode_z, NZ), edge]).astype(np.float32)
    twist = np.stack([twist.real, twist.imag]).astype(np.float32)
    return outer_real, twist, inner_real, inner_back, waves


def _exact(table):
    return np.asarray(table, np.float32).astype(ml_dtypes.bfloat16)


def _dot(left, right):
    return lax.dot_general(left, right, (((1,), (0,)), ((), ())), preferred_element_type=F32)


def _dot_nt(left, right):
    return lax.dot_general(left, right, (((1,), (1,)), ((), ())), preferred_element_type=F32)


def _split(value, count):
    out = []
    for i in range(count):
        piece = value.astype(BF16)
        out.append(piece)
        if i + 1 < count:
            value = value - piece.astype(F32)
    return out


VMEM = pl.BlockSpec(memory_space=pltpu.VMEM)
SMEM = pl.BlockSpec(memory_space=pltpu.SMEM)
ANY = pl.BlockSpec(memory_space=pl.ANY)


def _call(kernel, out_shape, in_specs, name, flops, nbytes, vmem, scratch_shapes=(), out_specs=None):
    return pl.pallas_call(
        kernel,
        out_shape=out_shape,
        in_specs=in_specs,
        out_specs=out_specs or jax.tree.map(lambda _: VMEM, out_shape),
        scratch_shapes=scratch_shapes,
        compiler_params=pltpu.CompilerParams(vmem_limit_bytes=vmem * MIB),
        cost_estimate=pl.CostEstimate(flops=flops, bytes_accessed=nbytes, transcendentals=0),
        name=name,
    )


def _odd(axis):
    return lax.rem(lax.axis_index(axis), 2)


def edges_kernel(state, y_first, y_second, y_first_heat, y_second_heat, z_first, z_second):
    odd_y, odd_z = _odd("gy"), _odd("gz")
    row = lax.broadcasted_iota(jnp.int32, (240, CELLS), 0)
    column = lax.broadcasted_iota(jnp.int32, (240, CELLS), 1)
    second = row >= 96
    within = jnp.where(second, row - 96, row)
    third = (within * 171) >> 9
    top_y = (BY - 3) * jnp.where(second, odd_y, 1 - odd_y)
    along_y = BY * third + (within - 3 * third) + top_y
    second = row >= 216
    top_z = (CELLS - 24) * jnp.where(second, odd_z, 1 - odd_z)
    along_z = jnp.where(second, row - 216, row - 192) + top_z
    source = jnp.where(row >= 192, along_z, along_y)
    pick = jnp.where(column == source, 1.0, 0.0).astype(BF16)
    for q in range(4):
        rows = _dot(pick, state[q])
        first, second, at = (y_first, y_second, q) if q < 3 else (y_first_heat, y_second_heat, 0)
        first[at] = rows[0:96].astype(BF16)
        second[at] = rows[96:192].astype(BF16)
        z_first[q] = rows[192:216].astype(BF16)
        z_second[q] = rows[216:240].astype(BF16)


def local_kernel(
    metric, strain, wave_x, state, along, waves, partial, partial_heat, carrier_y, carrier_z, factors
):
    along_x, along_y = along[:NX], along[NX:, :CELLS]
    speeds = [state[q].astype(F32) for q in range(4)]
    contra = [
        metric[0, j] * speeds[0] + metric[1, j] * speeds[1] + metric[2, j] * speeds[2]
        for j in range(3)
    ]
    scale = -STEP / 60.0
    carrier_y[...] = scale * contra[1]
    carrier_z[0:24] = scale * contra[2][0:24]
    carrier_z[24:48] = scale * contra[2][CELLS - 24 :]
    nothing = jnp.zeros((24, NX), F32)
    for q in range(4):
        d_x = _dot(state[q], along_x)
        d_y = _dot(along_y, state[q])
        tall = jnp.concatenate([nothing, speeds[q], nothing], axis=0)

        def moved(k):
            return tall[(3 + k) * BY : (3 + k) * BY + CELLS]

        d_z = (
            45.0 * (moved(1) - moved(-1)) - 9.0 * (moved(2) - moved(-2)) + (moved(3) - moved(-3))
        )
        carried = contra[0] * d_x + contra[1] * d_y + contra[2] * d_z
        if q < 3:
            rest = strain[q, 0] * speeds[0] + strain[q, 1] * speeds[1] + strain[q, 2] * speeds[2]
            if q == 2:
                rest = rest - speeds[3]
        else:
            rest = speeds[2]
        value = speeds[q] + scale * carried - STEP * rest
        if q < 3:
            partial[q] = value
        else:
            partial_heat[...] = value
    here = lax.axis_index("gy") * GZ + lax.axis_index("gz")
    wave_y, wave_z, edge = waves[0], waves[1], waves[2]
    for c in range(2):
        wx = wave_x[2 * here + c]
        symbol = jnp.zeros((DEV, CELLS), F32)
        for i in range(3):
            mixed = metric[i, 0] * wx + metric[i, 1] * wave_y + metric[i, 2] * wave_z
            symbol = symbol + mixed * mixed
        out = (edge * jnp.where(2 * here + c == 0, 1.0, 0.0)) > 0.5
        factors[c] = jnp.where(
            out, 0.0, -1.0 / (jnp.where(out, 1.0, symbol) * float(NX * NY * NZ))
        )


def _complete(partial, carrier_y, carrier_z, y_first, y_second, z_first, z_second, along_y, along_z):
    odd_y, odd_z = _odd("gy"), _odd("gz")
    beside = jnp.concatenate([y_first, y_second], axis=0)
    whole = partial + carrier_y[...] * _dot(along_y[odd_y], beside)
    first, second = _dot(along_z[odd_z], z_first), _dot(along_z[1 - odd_z], z_second)
    below = jnp.where(odd_z == 1, first, second)
    above = jnp.where(odd_z == 1, second, first)
    low = whole[:24] + carrier_z[0:24] * below
    high = whole[CELLS - 24 :] + carrier_z[24:48] * above
    return jnp.concatenate([low, whole[24 : CELLS - 24], high], axis=0)


def forward_kernel(
    metric,
    partial,
    carrier_y,
    carrier_z,
    y_first,
    y_second,
    z_first,
    z_second,
    along_y,
    along_z,
    spread,
    along_x,
    waves,
    provisional,
    sent,
):
    fields = [
        _complete(
            partial[q],
            carrier_y,
            carrier_z,
            y_first[q],
            y_second[q],
            z_first[q],
            z_second[q],
            along_y,
            along_z,
        )
        for q in range(3)
    ]
    for q in range(3):
        provisional[q] = fields[q]
    flux = [
        metric[0, j] * fields[0] + metric[1, j] * fields[1] + metric[2, j] * fields[2]
        for j in range(3)
    ]
    flux = [_split(f, 2) for f in flux]
    stacked = jnp.concatenate([flux[1][0], flux[2][0], flux[1][1], flux[2][1]], axis=0)
    own = _dot(jnp.concatenate(flux[0], axis=1), along_x[...])
    for part in range(EXT // CELLS):
        block = _dot(spread[part * CELLS : (part + 1) * CELLS], stacked)
        if part == 0:
            block = block + own
        high, low = _split(block, 2)
        spectrum = _dot_nt(waves[...], jnp.concatenate([high, high, low], axis=1))
        for t in range(CELLS // 128):
            at = 4 * (part * (CELLS // 128) + t)
            sent[:, at : at + 4, :] = spectrum[:, 128 * t : 128 * t + 128].reshape(DEV, 4, 128)


def plane_kernel(factors, got, outer, outer_back, twist, inner, inner_back, sent):
    chunks = EXT // 128
    parts = []
    for t in range(chunks):
        tr, ti = twist[0, :, 128 * t : 128 * t + 128], twist[1, :, 128 * t : 128 * t + 128]
        block = jnp.concatenate(
            [
                jnp.concatenate([got[:, 4 * t + 2 * c + part, :] for c in range(2)], axis=1)
                for part in range(2)
            ],
            axis=0,
        )
        high, low = _split(block, 2)
        block = _dot(outer[...], jnp.concatenate([high, high, low], axis=0))
        rows = []
        for c in range(2):
            at = slice(128 * c, 128 * c + 128)
            re, im = block[:DEV, at], block[DEV:, at]
            rows.append(jnp.concatenate([re * tr - im * ti, re * ti + im * tr], axis=1))
        high, low = _split(jnp.concatenate(rows, axis=0), 2)
        parts += [high, high, low]
    modes = _dot(jnp.concatenate(parts, axis=1), inner[...])
    solved = []
    for c in range(2):
        factor = factors[c]
        solved.append(modes[c * DEV : (c + 1) * DEV] * jnp.concatenate([factor, factor], axis=1))
    high, low = _split(jnp.concatenate(solved, axis=0), 2)
    left = jnp.concatenate([high] * 3 + [low] * 2, axis=1)
    every = _dot(left, inner_back[...])
    for t in range(chunks):
        tr, ti = twist[0, :, 128 * t : 128 * t + 128], twist[1, :, 128 * t : 128 * t + 128]
        cells = every[:, 256 * t : 256 * t + 256]
        columns = []
        for c in range(2):
            re, im = cells[c * DEV : (c + 1) * DEV, :128], cells[c * DEV : (c + 1) * DEV, 128:]
            columns.append(jnp.concatenate([re * tr + im * ti, im * tr - re * ti], axis=0))
        high, middle, low = _split(jnp.concatenate(columns, axis=1), 3)
        block = _dot(
            outer_back[...], jnp.concatenate([high] * 2 + [middle] * 2 + [low], axis=0)
        )
        for c in range(2):
            for part in range(2):
                sent[:, 4 * t + 2 * c + part, :] = block[
                    part * DEV : (part + 1) * DEV, 128 * c : 128 * c + 128
                ]


def project_kernel(
    metric,
    got,
    gather,
    inverse,
    symbol,
    provisional,
    partial,
    carrier_y,
    carrier_z,
    y_first,
    y_second,
    z_first,
    z_second,
    along_y,
    along_z,
    motion,
    heat,
    held,
    held_heat,
    done,
):
    held_heat[...] = _complete(
        partial[...],
        carrier_y,
        carrier_z,
        y_first[0],
        y_second[0],
        z_first[3],
        z_second[3],
        along_y,
        along_z,
    )
    copies = [pltpu.make_async_copy(held_heat, heat, done.at[3])]
    copies[0].start()
    pushes = [[], [], []]
    for c in range(2):
        block = jnp.concatenate(
            [
                jnp.concatenate([got[:, 4 * t + 2 * c + part, :] for t in range(EXT // 128)], axis=1)
                for part in range(2)
            ],
            axis=0,
        )
        fields = _dot_nt(gather[...], jnp.concatenate(_split(block, 3), axis=1))
        own, along_y, along_z = (fields[j * CELLS : (j + 1) * CELLS] for j in range(3))
        along_x = jnp.concatenate([-symbol[c] * own[:, 128:], symbol[c] * own[:, :128]], axis=1)
        for i in range(3):
            push = metric[i, 0] * along_x + metric[i, 1] * along_y + metric[i, 2] * along_z
            pushes[i].append(_split(push, 2))
    for i in range(3):
        (h0, l0), (h1, l1) = pushes[i]
        value = _dot(jnp.concatenate([h0, h0, h1, h1, l0, l1], axis=1), inverse[...])
        held[i] = provisional[i] - value
        copies.append(pltpu.make_async_copy(held.at[i], motion.at[i], done.at[i]))
        copies[-1].start()
    for copy in copies:
        copy.wait()


def _swaps(count):
    first = [(i, i ^ 1) for i in range(count)]
    second = [(i, (i + 1 if i % 2 else i - 1) % count) for i in range(count)]
    return first, second


def _step(state, metric, strain):
    along_y, along_z = _difference_matrices()
    forward, inverse, symbol = _x_tables()
    outer, twist, inner, inner_back, waves = _plane_tables()
    k = np.arange(NX // 2)
    wave_x = _kt(k, NX).astype(np.float32)
    wave_x[0] = 0.0
    circulant = _exact(_circulant_x())
    spread = _exact(-np.concatenate([along_y, along_z], axis=0).T)
    spread = np.concatenate([spread, spread], axis=1)
    gather = _exact(np.concatenate([np.eye(CELLS, EXT), along_y, along_z], axis=0))
    gather = np.concatenate([gather] * 3, axis=1)
    below, above = along_y[:, CELLS : CELLS + 96], along_y[:, CELLS + 96 : CELLS + 192]
    beside_y = _exact(
        np.stack([np.concatenate([above, below], axis=1), np.concatenate([below, above], axis=1)])
    )
    beside_z = _exact(
        np.stack([along_z[CELLS - 24 :, CELLS + 216 : CELLS + 240], along_z[:24, CELLS + 192 : CELLS + 216]])
    )
    local = np.zeros((NX + CELLS, NX))
    local[:NX] = _circulant_x()
    local[NX:, :CELLS] = along_y[:, :CELLS]

    field = jax.ShapeDtypeStruct((CELLS, NX), F32)
    fields = lambda count: jax.ShapeDtypeStruct((count, CELLS, NX), F32)
    block = jax.ShapeDtypeStruct((DEV, 16, 128), F32)
    state = state.reshape(4, CELLS, NX)

    y_side = jax.ShapeDtypeStruct((3, 96, NX), BF16)
    y_side_heat = jax.ShapeDtypeStruct((1, 96, NX), BF16)
    z_side = jax.ShapeDtypeStruct((4, 24, NX), BF16)
    y_first, y_second, y_first_heat, y_second_heat, z_first, z_second = _call(
        edges_kernel,
        (y_side, y_side, y_side_heat, y_side_heat, z_side, z_side),
        [VMEM],
        "edges",
        20_000_000_000,
        64 * MIB,
        16,
    )(state)
    swaps_y, swaps_z = _swaps(GY), _swaps(GZ)
    y_first = lax.ppermute(y_first, "gy", swaps_y[0])
    y_second = lax.ppermute(y_second, "gy", swaps_y[1])
    z_first = lax.ppermute(z_first, "gz", swaps_z[0])
    z_second = lax.ppermute(z_second, "gz", swaps_z[1])
    y_first_heat = lax.ppermute(y_first_heat, "gy", swaps_y[0])
    y_second_heat = lax.ppermute(y_second_heat, "gy", swaps_y[1])
    partial, partial_heat, carrier_y, carrier_z, factors = _call(
        local_kernel,
        (
            fields(3),
            field,
            field,
            jax.ShapeDtypeStruct((48, NX), F32),
            jax.ShapeDtypeStruct((2, DEV, CELLS), F32),
        ),
        [SMEM, SMEM, SMEM, VMEM, VMEM, VMEM],
        "local",
        1_000_000_000,
        4 * MIB,
        24,
    )(metric, strain, wave_x, state, _exact(local), waves)

    provisional, sent = _call(
        forward_kernel,
        (fields(3), block),
        [SMEM] + [VMEM] * 12,
        "forward",
        2_000_000_000,
        8 * MIB,
        40,
    )(
        metric,
        partial,
        carrier_y,
        carrier_z,
        y_first,
        y_second,
        z_first,
        z_second,
        beside_y,
        beside_z,
        spread,
        np.concatenate([circulant, circulant], axis=0),
        np.concatenate(_pieces(forward, 2)[[0, 1, 0]], axis=1),
    )
    sent, y_first_heat, y_second_heat = lax.optimization_barrier(
        (sent, y_first_heat, y_second_heat)
    )
    got = lax.all_to_all(sent, ("gy", "gz"), split_axis=0, concat_axis=0, tiled=True)
    sent = _call(
        plane_kernel, block, [VMEM] * 7, "plane", 3_600_000_000, 8 * MIB, 40
    )(
        factors,
        got,
        np.concatenate(_pieces(outer, 2)[[0, 1, 0]], axis=1),
        np.concatenate(_pieces(outer.T, 2)[[0, 1, 0, 1, 0]], axis=1),
        twist,
        inner,
        inner_back,
    )
    got = lax.all_to_all(sent, ("gy", "gz"), split_axis=0, concat_axis=0, tiled=True)
    motion, heat = _call(
        project_kernel,
        (fields(3), field),
        [SMEM] + [VMEM] * 14,
        "project",
        2_500_000_000,
        8 * MIB,
        40,
        out_specs=(ANY, ANY),
        scratch_shapes=[
            pltpu.VMEM((3, CELLS, NX), F32),
            pltpu.VMEM((CELLS, NX), F32),
            pltpu.SemaphoreType.DMA((4,)),
        ],
    )(
        metric,
        got,
        gather,
        inverse,
        symbol,
        provisional,
        partial_heat,
        carrier_y,
        carrier_z,
        y_first_heat,
        y_second_heat,
        z_first,
        z_second,
        beside_y,
        beside_z,
    )
    return motion.reshape(3, BZ, BY, NX), heat.reshape(BZ, BY, NX)


def solution(mesh):
    return jax.shard_map(
        _step,
        mesh=mesh,
        in_specs=(P(None, "gz", "gy", None), P(), P()),
        out_specs=(P(None, "gz", "gy", None), P("gz", "gy", None)),
        check_vma=False,
    )
```

```python
import numpy as np

import jax
import jax.numpy as jnp
import ml_dtypes
from jax import lax
from jax.experimental import pallas as pl
from jax.experimental.pallas import tpu as pltpu
from jax.sharding import PartitionSpec as P

F32 = jnp.float32
BF16 = jnp.bfloat16
NX, NY, NZ = 512, 256, 128
GY, GZ = 32, 4
BY, BZ = NY // GY, NZ // GZ
DEV = GY * GZ
CELLS = BY * BZ
EXT = 512
STEP = 0.4
COEF = {1: 45.0, -1: -45.0, 2: -9.0, -2: 9.0, 3: 1.0, -3: -1.0}
MIB = 1 << 20


def _pieces(table, count):
    rest = np.asarray(table, np.float64)
    out = []
    for _ in range(count):
        piece = rest.astype(np.float32).astype(ml_dtypes.bfloat16)
        out.append(piece)
        rest = rest - piece.astype(np.float64)
    return np.stack(out)


def _ext_cells():
    cells = [(w, y) for w in range(BZ) for y in range(BY)]
    cells += [(w, y) for w in range(BZ) for y in range(-3, 0)]
    cells += [(w, y) for w in range(BZ) for y in range(BY, BY + 3)]
    cells += [(w, y) for w in range(-3, 0) for y in range(BY)]
    cells += [(w, y) for w in range(BZ, BZ + 3) for y in range(BY)]
    return cells


def _difference_matrices():
    place = {cell: i for i, cell in enumerate(_ext_cells())}
    along_y = np.zeros((CELLS, EXT))
    along_z = np.zeros((CELLS, EXT))
    for w in range(BZ):
        for y in range(BY):
            row = place[(w, y)]
            for k, c in COEF.items():
                along_y[row, place[(w, y + k)]] = c
                along_z[row, place[(w + k, y)]] = c
    return along_y, along_z


def _circulant_x():
    table = np.zeros((NX, NX))
    for x in range(NX):
        for k, c in COEF.items():
            table[(x + k) % NX, x] = c
    return table


def _kt(modes, length):
    a = 2.0 * np.pi * modes / length
    return 1.5 * np.sin(a) - 0.3 * np.sin(2 * a) + np.sin(3 * a) / 30.0


def _x_tables():
    k = np.arange(NX // 2)[:, None]
    x = np.arange(NX)[None, :]
    angle = 2.0 * np.pi * ((k * x) % NX) / NX
    alternating = 1.0 - 2.0 * (np.arange(NX) % 2)
    forward = np.zeros((NX // 2, 2, NX))
    forward[:, 0], forward[:, 1] = np.cos(angle), -np.sin(angle)
    forward[0, 0], forward[0, 1] = 1.0, alternating
    inverse = 2.0 * forward
    inverse[0] = forward[0]
    inverse = inverse.reshape(DEV, 2, 2, NX).transpose(1, 2, 0, 3).reshape(2, 2 * DEV, NX)
    symbol = 60.0 * _kt(np.arange(NX // 2), NX)
    symbol[0] = 0.0
    symbol = symbol.reshape(DEV, 2).T.reshape(2, 1, DEV).astype(np.float32)
    inverse = _pieces(inverse / 60.0, 2)
    inverse = np.concatenate(
        [inverse[0, 0], inverse[1, 0], inverse[0, 1], inverse[1, 1], inverse[0, 0], inverse[0, 1]]
    )
    return forward.reshape(NX, NX) / 60.0, inverse, symbol


def _plane_tables():
    a = np.arange(DEV)
    m1, n1 = a // GZ, a % GZ
    gy, gz = a // GZ, a % GZ
    outer = np.exp(
        -2j * np.pi * (np.outer(m1, gy) / GY + np.outer(n1, gz) / GZ)
    )
    cells = np.array(_ext_cells())
    count = len(cells)
    w, y = cells[:, 0], cells[:, 1]
    twist = np.zeros((DEV, EXT), complex)
    twist[:, :count] = np.exp(-2j * np.pi * (np.outer(n1, w) / NZ + np.outer(m1, y) / NY))
    b = np.arange(CELLS)
    n2, m2 = b // BY, b % BY
    inner = np.zeros((EXT, CELLS), complex)
    inner[:count] = np.exp(-2j * np.pi * (np.outer(w, n2) / BZ + np.outer(y, m2) / BY))
    outer_real = np.block([[outer.real, -outer.imag], [outer.imag, outer.real]])
    inner_real = np.block([[inner.real, inner.imag], [-inner.imag, inner.real]])
    chunks = EXT // 128
    inner_back = _pieces(inner_real.T, 3)[[0, 1, 2, 0, 1]].reshape(5, 2 * CELLS, 2, chunks, 128)
    inner_back = inner_back.transpose(0, 1, 3, 2, 4).reshape(10 * CELLS, 1024)
    inner_real = _pieces(inner_real, 2)[[0, 1, 0]].reshape(3, 2, chunks, 128, 2 * CELLS)
    inner_real = inner_real.transpose(2, 0, 1, 3, 4).reshape(chunks * 768, 2 * CELLS)
    mode_y = m1[:, None] + GY * m2[None, :]
    mode_z = n1[:, None] + GZ * n2[None, :]
    edge = (((2 * mode_y) % NY == 0) & ((2 * mode_z) % NZ == 0)).astype(np.float32)
    waves = np.stack([_kt(mode_y, NY), _kt(mode_z, NZ), edge]).astype(np.float32)
    twist = np.stack([twist.real, twist.imag]).astype(np.float32)
    return outer_real, twist, inner_real, inner_back, waves


def _exact(table):
    return np.asarray(table, np.float32).astype(ml_dtypes.bfloat16)


def _dot(left, right):
    return lax.dot_general(left, right, (((1,), (0,)), ((), ())), preferred_element_type=F32)


def _dot_nt(left, right):
    return lax.dot_general(left, right, (((1,), (1,)), ((), ())), preferred_element_type=F32)


def _split(value, count):
    out = []
    for i in range(count):
        piece = value.astype(BF16)
        out.append(piece)
        if i + 1 < count:
            value = value - piece.astype(F32)
    return out


VMEM = pl.BlockSpec(memory_space=pltpu.VMEM)
SMEM = pl.BlockSpec(memory_space=pltpu.SMEM)
ANY = pl.BlockSpec(memory_space=pl.ANY)


def _call(kernel, out_shape, in_specs, name, flops, nbytes, vmem, scratch_shapes=(), out_specs=None):
    return pl.pallas_call(
        kernel,
        out_shape=out_shape,
        in_specs=in_specs,
        out_specs=out_specs or jax.tree.map(lambda _: VMEM, out_shape),
        scratch_shapes=scratch_shapes,
        compiler_params=pltpu.CompilerParams(vmem_limit_bytes=vmem * MIB),
        cost_estimate=pl.CostEstimate(flops=flops, bytes_accessed=nbytes, transcendentals=0),
        name=name,
    )


def _odd(axis):
    return lax.rem(lax.axis_index(axis), 2)


def edges_kernel(state, y_first, y_second, y_first_heat, y_second_heat, z_first, z_second):
    odd_y, odd_z = _odd("gy"), _odd("gz")
    row = lax.broadcasted_iota(jnp.int32, (240, CELLS), 0)
    column = lax.broadcasted_iota(jnp.int32, (240, CELLS), 1)
    second = row >= 96
    within = jnp.where(second, row - 96, row)
    third = (within * 171) >> 9
    top_y = (BY - 3) * jnp.where(second, odd_y, 1 - odd_y)
    along_y = BY * third + (within - 3 * third) + top_y
    second = row >= 216
    top_z = (CELLS - 24) * jnp.where(second, odd_z, 1 - odd_z)
    along_z = jnp.where(second, row - 216, row - 192) + top_z
    source = jnp.where(row >= 192, along_z, along_y)
    pick = jnp.where(column == source, 1.0, 0.0).astype(BF16)
    for q in range(4):
        rows = _dot(pick, state[q])
        first, second, at = (y_first, y_second, q) if q < 3 else (y_first_heat, y_second_heat, 0)
        first[at] = rows[0:96].astype(BF16)
        second[at] = rows[96:192].astype(BF16)
        z_first[q] = rows[192:216].astype(BF16)
        z_second[q] = rows[216:240].astype(BF16)


def local_kernel(
    metric, strain, wave_x, state, along, waves, partial, partial_heat, carrier_y, carrier_z, factors
):
    along_x, along_y = along[:NX], along[NX:, :CELLS]
    speeds = [state[q].astype(F32) for q in range(4)]
    contra = [
        metric[0, j] * speeds[0] + metric[1, j] * speeds[1] + metric[2, j] * speeds[2]
        for j in range(3)
    ]
    scale = -STEP / 60.0
    carrier_y[...] = scale * contra[1]
    carrier_z[0:24] = scale * contra[2][0:24]
    carrier_z[24:48] = scale * contra[2][CELLS - 24 :]
    nothing = jnp.zeros((24, NX), F32)
    for q in range(4):
        d_x = _dot(state[q], along_x)
        d_y = _dot(along_y, state[q])
        tall = jnp.concatenate([nothing, speeds[q], nothing], axis=0)

        def moved(k):
            return tall[(3 + k) * BY : (3 + k) * BY + CELLS]

        d_z = (
            45.0 * (moved(1) - moved(-1)) - 9.0 * (moved(2) - moved(-2)) + (moved(3) - moved(-3))
        )
        carried = contra[0] * d_x + contra[1] * d_y + contra[2] * d_z
        if q < 3:
            rest = strain[q, 0] * speeds[0] + strain[q, 1] * speeds[1] + strain[q, 2] * speeds[2]
            if q == 2:
                rest = rest - speeds[3]
        else:
            rest = speeds[2]
        value = speeds[q] + scale * carried - STEP * rest
        if q < 3:
            partial[q] = value
        else:
            partial_heat[...] = value
    here = lax.axis_index("gy") * GZ + lax.axis_index("gz")
    wave_y, wave_z, edge = waves[0], waves[1], waves[2]
    for c in range(2):
        wx = wave_x[2 * here + c]
        symbol = jnp.zeros((DEV, CELLS), F32)
        for i in range(3):
            mixed = metric[i, 0] * wx + metric[i, 1] * wave_y + metric[i, 2] * wave_z
            symbol = symbol + mixed * mixed
        out = (edge * jnp.where(2 * here + c == 0, 1.0, 0.0)) > 0.5
        factors[c] = jnp.where(
            out, 0.0, -1.0 / (jnp.where(out, 1.0, symbol) * float(NX * NY * NZ))
        )


def _complete(partial, carrier_y, carrier_z, y_first, y_second, z_first, z_second, along_y, along_z):
    odd_y, odd_z = _odd("gy"), _odd("gz")
    beside = jnp.concatenate([y_first, y_second], axis=0)
    whole = partial + carrier_y[...] * _dot(along_y[odd_y], beside)
    first, second = _dot(along_z[odd_z], z_first), _dot(along_z[1 - odd_z], z_second)
    below = jnp.where(odd_z == 1, first, second)
    above = jnp.where(odd_z == 1, second, first)
    low = whole[:24] + carrier_z[0:24] * below
    high = whole[CELLS - 24 :] + carrier_z[24:48] * above
    return jnp.concatenate([low, whole[24 : CELLS - 24], high], axis=0)


def forward_kernel(
    metric,
    partial,
    carrier_y,
    carrier_z,
    y_first,
    y_second,
    z_first,
    z_second,
    along_y,
    along_z,
    spread,
    along_x,
    waves,
    provisional,
    sent,
):
    fields = [
        _complete(
            partial[q],
            carrier_y,
            carrier_z,
            y_first[q],
            y_second[q],
            z_first[q],
            z_second[q],
            along_y,
            along_z,
        )
        for q in range(3)
    ]
    for q in range(3):
        provisional[q] = fields[q]
    flux = [
        metric[0, j] * fields[0] + metric[1, j] * fields[1] + metric[2, j] * fields[2]
        for j in range(3)
    ]
    flux = [_split(f, 2) for f in flux]
    stacked = [jnp.concatenate(flux[j], axis=0) for j in (1, 2)]
    own = _dot(jnp.concatenate(flux[0], axis=1), along_x[...])
    for part in range(EXT // CELLS):
        if part == 0:
            block = own + _dot(spread[:CELLS], jnp.concatenate(stacked, axis=0))
        else:
            beside_y = _dot(spread[CELLS : CELLS + 192, :NX], stacked[0])
            beside_z = _dot(spread[CELLS + 192 :, NX:], stacked[1])
            block = jnp.concatenate([beside_y, beside_z], axis=0)
        high, low = _split(block, 2)
        spectrum = _dot_nt(waves[...], jnp.concatenate([high, high, low], axis=1))
        for t in range(CELLS // 128):
            at = 4 * (part * (CELLS // 128) + t)
            sent[:, at : at + 4, :] = spectrum[:, 128 * t : 128 * t + 128].reshape(DEV, 4, 128)


def plane_kernel(factors, got, outer, outer_back, twist, inner, inner_back, sent):
    chunks = EXT // 128
    parts = []
    for t in range(chunks):
        tr, ti = twist[0, :, 128 * t : 128 * t + 128], twist[1, :, 128 * t : 128 * t + 128]
        block = jnp.concatenate(
            [
                jnp.concatenate([got[:, 4 * t + 2 * c + part, :] for c in range(2)], axis=1)
                for part in range(2)
            ],
            axis=0,
        )
        high, low = _split(block, 2)
        block = _dot(outer[...], jnp.concatenate([high, high, low], axis=0))
        rows = []
        for c in range(2):
            at = slice(128 * c, 128 * c + 128)
            re, im = block[:DEV, at], block[DEV:, at]
            rows.append(jnp.concatenate([re * tr - im * ti, re * ti + im * tr], axis=1))
        high, low = _split(jnp.concatenate(rows, axis=0), 2)
        parts += [high, high, low]
    modes = _dot(jnp.concatenate(parts, axis=1), inner[...])
    solved = []
    for c in range(2):
        factor = factors[c]
        solved.append(modes[c * DEV : (c + 1) * DEV] * jnp.concatenate([factor, factor], axis=1))
    high, low = _split(jnp.concatenate(solved, axis=0), 2)
    left = jnp.concatenate([high] * 3 + [low] * 2, axis=1)
    every = _dot(left, inner_back[...])
    for t in range(chunks):
        tr, ti = twist[0, :, 128 * t : 128 * t + 128], twist[1, :, 128 * t : 128 * t + 128]
        cells = every[:, 256 * t : 256 * t + 256]
        columns = []
        for c in range(2):
            re, im = cells[c * DEV : (c + 1) * DEV, :128], cells[c * DEV : (c + 1) * DEV, 128:]
            columns.append(jnp.concatenate([re * tr + im * ti, im * tr - re * ti], axis=0))
        high, middle, low = _split(jnp.concatenate(columns, axis=1), 3)
        block = _dot(
            outer_back[...], jnp.concatenate([high] * 2 + [middle] * 2 + [low], axis=0)
        )
        for c in range(2):
            for part in range(2):
                sent[:, 4 * t + 2 * c + part, :] = block[
                    part * DEV : (part + 1) * DEV, 128 * c : 128 * c + 128
                ]


def project_kernel(
    metric,
    got,
    gather,
    keep,
    inverse,
    symbol,
    provisional,
    partial,
    carrier_y,
    carrier_z,
    y_first,
    y_second,
    z_first,
    z_second,
    along_y,
    along_z,
    motion,
    heat,
    held,
    held_heat,
    done,
):
    held_heat[...] = _complete(
        partial[...],
        carrier_y,
        carrier_z,
        y_first[0],
        y_second[0],
        z_first[3],
        z_second[3],
        along_y,
        along_z,
    )
    copies = [pltpu.make_async_copy(held_heat, heat, done.at[3])]
    copies[0].start()
    pushes = [[], [], []]
    for c in range(2):
        block = jnp.concatenate(
            [
                jnp.concatenate([got[:, 4 * t + 2 * c + part, :] for t in range(EXT // 128)], axis=1)
                for part in range(2)
            ],
            axis=0,
        )
        split = _split(block, 3)
        fields = _dot_nt(gather[...], jnp.concatenate(split, axis=1))
        along_y, along_z = fields[:CELLS], fields[CELLS:]
        own = _dot_nt(keep[...], jnp.concatenate([p[:, :CELLS] for p in split[:2]], axis=1))
        along_x = jnp.concatenate([-symbol[c] * own[:, 128:], symbol[c] * own[:, :128]], axis=1)
        for i in range(3):
            push = metric[i, 0] * along_x + metric[i, 1] * along_y + metric[i, 2] * along_z
            pushes[i].append(_split(push, 2))
    for i in range(3):
        (h0, l0), (h1, l1) = pushes[i]
        value = _dot(jnp.concatenate([h0, h0, h1, h1, l0, l1], axis=1), inverse[...])
        held[i] = provisional[i] - value
        copies.append(pltpu.make_async_copy(held.at[i], motion.at[i], done.at[i]))
        copies[-1].start()
    for copy in copies:
        copy.wait()


def _swaps(count):
    first = [(i, i ^ 1) for i in range(count)]
    second = [(i, (i + 1 if i % 2 else i - 1) % count) for i in range(count)]
    return first, second


def _step(state, metric, strain):
    along_y, along_z = _difference_matrices()
    forward, inverse, symbol = _x_tables()
    outer, twist, inner, inner_back, waves = _plane_tables()
    k = np.arange(NX // 2)
    wave_x = _kt(k, NX).astype(np.float32)
    wave_x[0] = 0.0
    circulant = _exact(_circulant_x())
    spread = _exact(-np.concatenate([along_y, along_y, along_z, along_z], axis=0).T)
    gather = _exact(np.concatenate([along_y, along_z], axis=0))
    keep = _exact(np.concatenate([np.eye(CELLS)] * 2, axis=1))
    gather = np.concatenate([gather] * 3, axis=1)
    below, above = along_y[:, CELLS : CELLS + 96], along_y[:, CELLS + 96 : CELLS + 192]
    beside_y = _exact(
        np.stack([np.concatenate([above, below], axis=1), np.concatenate([below, above], axis=1)])
    )
    beside_z = _exact(
        np.stack([along_z[CELLS - 24 :, CELLS + 216 : CELLS + 240], along_z[:24, CELLS + 192 : CELLS + 216]])
    )
    local = np.zeros((NX + CELLS, NX))
    local[:NX] = _circulant_x()
    local[NX:, :CELLS] = along_y[:, :CELLS]

    field = jax.ShapeDtypeStruct((CELLS, NX), F32)
    fields = lambda count: jax.ShapeDtypeStruct((count, CELLS, NX), F32)
    block = jax.ShapeDtypeStruct((DEV, 16, 128), F32)
    state = state.reshape(4, CELLS, NX)

    y_side = jax.ShapeDtypeStruct((3, 96, NX), BF16)
    y_side_heat = jax.ShapeDtypeStruct((1, 96, NX), BF16)
    z_side = jax.ShapeDtypeStruct((4, 24, NX), BF16)
    y_first, y_second, y_first_heat, y_second_heat, z_first, z_second = _call(
        edges_kernel,
        (y_side, y_side, y_side_heat, y_side_heat, z_side, z_side),
        [VMEM],
        "edges",
        20_000_000_000,
        64 * MIB,
        16,
    )(state)
    swaps_y, swaps_z = _swaps(GY), _swaps(GZ)
    y_first = lax.ppermute(y_first, "gy", swaps_y[0])
    y_second = lax.ppermute(y_second, "gy", swaps_y[1])
    z_first = lax.ppermute(z_first, "gz", swaps_z[0])
    z_second = lax.ppermute(z_second, "gz", swaps_z[1])
    partial, partial_heat, carrier_y, carrier_z, factors = _call(
        local_kernel,
        (
            fields(3),
            field,
            field,
            jax.ShapeDtypeStruct((48, NX), F32),
            jax.ShapeDtypeStruct((2, DEV, CELLS), F32),
        ),
        [SMEM, SMEM, SMEM, VMEM, VMEM, VMEM],
        "local",
        1_000_000_000,
        4 * MIB,
        24,
    )(metric, strain, wave_x, state, _exact(local), waves)

    y_first_heat, y_second_heat, carrier_z = lax.optimization_barrier(
        (y_first_heat, y_second_heat, carrier_z)
    )
    y_first_heat = lax.ppermute(y_first_heat, "gy", swaps_y[0])
    y_second_heat = lax.ppermute(y_second_heat, "gy", swaps_y[1])
    provisional, sent = _call(
        forward_kernel,
        (fields(3), block),
        [SMEM] + [VMEM] * 12,
        "forward",
        2_000_000_000,
        8 * MIB,
        40,
    )(
        metric,
        partial,
        carrier_y,
        carrier_z,
        y_first,
        y_second,
        z_first,
        z_second,
        beside_y,
        beside_z,
        spread,
        np.concatenate([circulant, circulant], axis=0),
        np.concatenate(_pieces(forward, 2)[[0, 1, 0]], axis=1),
    )
    sent, y_first_heat, y_second_heat = lax.optimization_barrier(
        (sent, y_first_heat, y_second_heat)
    )
    got = lax.all_to_all(sent, ("gy", "gz"), split_axis=0, concat_axis=0, tiled=True)
    sent = _call(
        plane_kernel, block, [VMEM] * 7, "plane", 3_600_000_000, 8 * MIB, 40
    )(
        factors,
        got,
        np.concatenate(_pieces(outer, 2)[[0, 1, 0]], axis=1),
        np.concatenate(_pieces(outer.T, 2)[[0, 1, 0, 1, 0]], axis=1),
        twist,
        inner,
        inner_back,
    )
    got = lax.all_to_all(sent, ("gy", "gz"), split_axis=0, concat_axis=0, tiled=True)
    motion, heat = _call(
        project_kernel,
        (fields(3), field),
        [SMEM] + [VMEM] * 15,
        "project",
        2_500_000_000,
        8 * MIB,
        40,
        out_specs=(ANY, ANY),
        scratch_shapes=[
            pltpu.VMEM((3, CELLS, NX), F32),
            pltpu.VMEM((CELLS, NX), F32),
            pltpu.SemaphoreType.DMA((4,)),
        ],
    )(
        metric,
        got,
        gather,
        keep,
        inverse,
        symbol,
        provisional,
        partial_heat,
        carrier_y,
        carrier_z,
        y_first_heat,
        y_second_heat,
        z_first,
        z_second,
        beside_y,
        beside_z,
    )
    return motion.reshape(3, BZ, BY, NX), heat.reshape(BZ, BY, NX)


def solution(mesh):
    return jax.shard_map(
        _step,
        mesh=mesh,
        in_specs=(P(None, "gz", "gy", None), P(), P()),
        out_specs=(P(None, "gz", "gy", None), P("gz", "gy", None)),
        check_vma=False,
    )
```

```python
import numpy as np

import jax
import jax.numpy as jnp
import ml_dtypes
from jax import lax
from jax.experimental import pallas as pl
from jax.experimental.pallas import tpu as pltpu
from jax.sharding import PartitionSpec as P

F32 = jnp.float32
BF16 = jnp.bfloat16
NX, NY, NZ = 512, 256, 128
GY, GZ = 32, 4
BY, BZ = NY // GY, NZ // GZ
DEV = GY * GZ
CELLS = BY * BZ
EXT = 512
STEP = 0.4
COEF = {1: 45.0, -1: -45.0, 2: -9.0, -2: 9.0, 3: 1.0, -3: -1.0}
MIB = 1 << 20


def _pieces(table, count):
    rest = np.asarray(table, np.float64)
    out = []
    for _ in range(count):
        piece = rest.astype(np.float32).astype(ml_dtypes.bfloat16)
        out.append(piece)
        rest = rest - piece.astype(np.float64)
    return np.stack(out)


def _ext_cells():
    cells = [(w, y) for w in range(BZ) for y in range(BY)]
    cells += [(w, y) for w in range(BZ) for y in range(-3, 0)]
    cells += [(w, y) for w in range(BZ) for y in range(BY, BY + 3)]
    cells += [(w, y) for w in range(-3, 0) for y in range(BY)]
    cells += [(w, y) for w in range(BZ, BZ + 3) for y in range(BY)]
    return cells


def _difference_matrices():
    place = {cell: i for i, cell in enumerate(_ext_cells())}
    along_y = np.zeros((CELLS, EXT))
    along_z = np.zeros((CELLS, EXT))
    for w in range(BZ):
        for y in range(BY):
            row = place[(w, y)]
            for k, c in COEF.items():
                along_y[row, place[(w, y + k)]] = c
                along_z[row, place[(w + k, y)]] = c
    return along_y, along_z


def _circulant_x():
    table = np.zeros((NX, NX))
    for x in range(NX):
        for k, c in COEF.items():
            table[(x + k) % NX, x] = c
    return table


def _kt(modes, length):
    a = 2.0 * np.pi * modes / length
    return 1.5 * np.sin(a) - 0.3 * np.sin(2 * a) + np.sin(3 * a) / 30.0


def _x_tables():
    k = np.arange(NX // 2)[:, None]
    x = np.arange(NX)[None, :]
    angle = 2.0 * np.pi * ((k * x) % NX) / NX
    alternating = 1.0 - 2.0 * (np.arange(NX) % 2)
    forward = np.zeros((NX // 2, 2, NX))
    forward[:, 0], forward[:, 1] = np.cos(angle), -np.sin(angle)
    forward[0, 0], forward[0, 1] = 1.0, alternating
    inverse = 2.0 * forward
    inverse[0] = forward[0]
    inverse = inverse.reshape(DEV, 2, 2, NX).transpose(1, 2, 0, 3).reshape(2, 2 * DEV, NX)
    symbol = 60.0 * _kt(np.arange(NX // 2), NX)
    symbol[0] = 0.0
    symbol = symbol.reshape(DEV, 2).T.reshape(2, 1, DEV).astype(np.float32)
    inverse = _pieces(inverse / 60.0, 2)
    inverse = np.concatenate(
        [inverse[0, 0], inverse[1, 0], inverse[0, 1], inverse[1, 1], inverse[0, 0], inverse[0, 1]]
    )
    return forward.reshape(NX, NX) / 60.0, inverse, symbol


def _plane_tables():
    a = np.arange(DEV)
    m1, n1 = a // GZ, a % GZ
    gy, gz = a // GZ, a % GZ
    outer = np.exp(
        -2j * np.pi * (np.outer(m1, gy) / GY + np.outer(n1, gz) / GZ)
    )
    cells = np.array(_ext_cells())
    count = len(cells)
    w, y = cells[:, 0], cells[:, 1]
    twist = np.zeros((DEV, EXT), complex)
    twist[:, :count] = np.exp(-2j * np.pi * (np.outer(n1, w) / NZ + np.outer(m1, y) / NY))
    b = np.arange(CELLS)
    n2, m2 = b // BY, b % BY
    inner = np.zeros((EXT, CELLS), complex)
    inner[:count] = np.exp(-2j * np.pi * (np.outer(w, n2) / BZ + np.outer(y, m2) / BY))
    outer_real = np.block([[outer.real, -outer.imag], [outer.imag, outer.real]])
    inner_real = np.block([[inner.real, inner.imag], [-inner.imag, inner.real]])
    chunks = EXT // 128
    inner_back = _pieces(inner_real.T, 3)[[0, 1, 2, 0, 1]].reshape(5, 2 * CELLS, 2, chunks, 128)
    inner_back = inner_back.transpose(0, 1, 3, 2, 4).reshape(10 * CELLS, 1024)
    inner_real = _pieces(inner_real, 2)[[0, 1, 0]].reshape(3, 2, chunks, 128, 2 * CELLS)
    inner_real = inner_real.transpose(2, 0, 1, 3, 4).reshape(chunks * 768, 2 * CELLS)
    mode_y = m1[:, None] + GY * m2[None, :]
    mode_z = n1[:, None] + GZ * n2[None, :]
    edge = (((2 * mode_y) % NY == 0) & ((2 * mode_z) % NZ == 0)).astype(np.float32)
    waves = np.stack([_kt(mode_y, NY), _kt(mode_z, NZ), edge]).astype(np.float32)
    twist = np.stack([twist.real, twist.imag]).astype(np.float32)
    return outer_real, twist, inner_real, inner_back, waves


def _exact(table):
    return np.asarray(table, np.float32).astype(ml_dtypes.bfloat16)


def _dot(left, right):
    return lax.dot_general(left, right, (((1,), (0,)), ((), ())), preferred_element_type=F32)


def _dot_nt(left, right):
    return lax.dot_general(left, right, (((1,), (1,)), ((), ())), preferred_element_type=F32)


def _split(value, count):
    out = []
    for i in range(count):
        piece = value.astype(BF16)
        out.append(piece)
        if i + 1 < count:
            value = value - piece.astype(F32)
    return out


VMEM = pl.BlockSpec(memory_space=pltpu.VMEM)
SMEM = pl.BlockSpec(memory_space=pltpu.SMEM)
ANY = pl.BlockSpec(memory_space=pl.ANY)


def _call(kernel, out_shape, in_specs, name, flops, nbytes, vmem, scratch_shapes=(), out_specs=None):
    return pl.pallas_call(
        kernel,
        out_shape=out_shape,
        in_specs=in_specs,
        out_specs=out_specs or jax.tree.map(lambda _: VMEM, out_shape),
        scratch_shapes=scratch_shapes,
        compiler_params=pltpu.CompilerParams(vmem_limit_bytes=vmem * MIB),
        cost_estimate=pl.CostEstimate(flops=flops, bytes_accessed=nbytes, transcendentals=0),
        name=name,
    )


def _odd(axis):
    return lax.rem(lax.axis_index(axis), 2)


def edges_kernel(state, y_first, y_second, y_first_heat, y_second_heat, z_first, z_second):
    odd_y, odd_z = _odd("gy"), _odd("gz")
    row = lax.broadcasted_iota(jnp.int32, (240, CELLS), 0)
    column = lax.broadcasted_iota(jnp.int32, (240, CELLS), 1)
    second = row >= 96
    within = jnp.where(second, row - 96, row)
    third = (within * 171) >> 9
    top_y = (BY - 3) * jnp.where(second, odd_y, 1 - odd_y)
    along_y = BY * third + (within - 3 * third) + top_y
    second = row >= 216
    top_z = (CELLS - 24) * jnp.where(second, odd_z, 1 - odd_z)
    along_z = jnp.where(second, row - 216, row - 192) + top_z
    source = jnp.where(row >= 192, along_z, along_y)
    pick = jnp.where(column == source, 1.0, 0.0).astype(BF16)
    for q in range(4):
        rows = _dot(pick, state[q])
        first, second, at = (y_first, y_second, q) if q < 3 else (y_first_heat, y_second_heat, 0)
        first[at] = rows[0:96].astype(BF16)
        second[at] = rows[96:192].astype(BF16)
        z_first[q] = rows[192:216].astype(BF16)
        z_second[q] = rows[216:240].astype(BF16)


def local_kernel(
    metric, strain, wave_x, state, along, waves, partial, partial_heat, carrier_y, carrier_z, carrier_second, factors
):
    along_x, along_y = along[:NX], along[NX:, :CELLS]
    speeds = [state[q].astype(F32) for q in range(4)]
    contra = [
        metric[0, j] * speeds[0] + metric[1, j] * speeds[1] + metric[2, j] * speeds[2]
        for j in range(3)
    ]
    scale = -STEP / 60.0
    carrier_y[...] = scale * contra[1]
    row = lax.broadcasted_iota(jnp.int32, (96, CELLS), 0)
    column = lax.broadcasted_iota(jnp.int32, (96, CELLS), 1)
    third = (row * 171) >> 9
    source = BY * third + (row - 3 * third) + (BY - 3) * _odd("gy")
    pick = jnp.where(column == source, 1.0, 0.0).astype(BF16)
    high, middle, low = _split(scale * contra[1], 3)
    carrier_second[...] = (_dot(pick, low) + _dot(pick, middle)) + _dot(pick, high)
    carrier_z[0:24] = scale * contra[2][0:24]
    carrier_z[24:48] = scale * contra[2][CELLS - 24 :]
    nothing = jnp.zeros((24, NX), F32)
    for q in range(4):
        d_x = _dot(state[q], along_x)
        d_y = _dot(along_y, state[q])
        tall = jnp.concatenate([nothing, speeds[q], nothing], axis=0)

        def moved(k):
            return tall[(3 + k) * BY : (3 + k) * BY + CELLS]

        d_z = (
            45.0 * (moved(1) - moved(-1)) - 9.0 * (moved(2) - moved(-2)) + (moved(3) - moved(-3))
        )
        carried = contra[0] * d_x + contra[1] * d_y + contra[2] * d_z
        if q < 3:
            rest = strain[q, 0] * speeds[0] + strain[q, 1] * speeds[1] + strain[q, 2] * speeds[2]
            if q == 2:
                rest = rest - speeds[3]
        else:
            rest = speeds[2]
        value = speeds[q] + scale * carried - STEP * rest
        if q < 3:
            partial[q] = value
        else:
            partial_heat[...] = value
    here = lax.axis_index("gy") * GZ + lax.axis_index("gz")
    wave_y, wave_z, edge = waves[0], waves[1], waves[2]
    for c in range(2):
        wx = wave_x[2 * here + c]
        symbol = jnp.zeros((DEV, CELLS), F32)
        for i in range(3):
            mixed = metric[i, 0] * wx + metric[i, 1] * wave_y + metric[i, 2] * wave_z
            symbol = symbol + mixed * mixed
        out = (edge * jnp.where(2 * here + c == 0, 1.0, 0.0)) > 0.5
        factors[c] = jnp.where(
            out, 0.0, -1.0 / (jnp.where(out, 1.0, symbol) * float(NX * NY * NZ))
        )


def _with_z(whole, carrier_z, z_first, z_second, along_z):
    odd = _odd("gz")
    first, second = _dot(along_z[odd], z_first), _dot(along_z[1 - odd], z_second)
    below = jnp.where(odd == 1, first, second)
    above = jnp.where(odd == 1, second, first)
    low = whole[:24] + carrier_z[0:24] * below
    high = whole[CELLS - 24 :] + carrier_z[24:48] * above
    return jnp.concatenate([low, whole[24 : CELLS - 24], high], axis=0)


def _flux(metric, fields):
    return [
        metric[0, j] * fields[0] + metric[1, j] * fields[1] + metric[2, j] * fields[2]
        for j in range(3)
    ]


def early_kernel(
    metric,
    partial,
    carrier_y,
    carrier_z,
    y_first,
    z_first,
    along_first,
    along_z,
    spread,
    along_x,
    waves,
    provisional,
    spectrum,
):
    odd, odd_z = _odd("gy"), _odd("gz")
    fields = []
    for q in range(3):
        whole = partial[q] + carrier_y[...] * _dot(along_first[odd], y_first[q])
        first = _dot(along_z[odd_z], z_first[q])
        low = whole[:24] + carrier_z[0:24] * jnp.where(odd_z == 1, first, 0.0)
        high = whole[CELLS - 24 :] + carrier_z[24:48] * jnp.where(odd_z == 1, 0.0, first)
        fields.append(jnp.concatenate([low, whole[24 : CELLS - 24], high], axis=0))
        provisional[q] = fields[q]
    flux = [_split(f, 2) for f in _flux(metric, fields)]
    stacked = [jnp.concatenate(flux[j], axis=0) for j in (1, 2)]
    own = _dot(jnp.concatenate(flux[0], axis=1), along_x[...])
    for part in range(EXT // CELLS):
        if part == 0:
            block = own + _dot(spread[:CELLS], jnp.concatenate(stacked, axis=0))
        else:
            beside_y = _dot(spread[CELLS : CELLS + 192, :NX], stacked[0])
            beside_z = _dot(spread[CELLS + 192 :, NX:], stacked[1])
            block = jnp.concatenate([beside_y, beside_z], axis=0)
        high, low = _split(block, 2)
        spectrum[:, part * CELLS : (part + 1) * CELLS] = _dot_nt(
            waves[...], jnp.concatenate([high, high, low], axis=1)
        )


def forward_kernel(
    metric,
    partial,
    spectrum,
    carrier_y,
    carrier_z,
    carrier_second,
    y_second,
    z_second,
    along_second,
    along_rows,
    along_z,
    spread_rows,
    along_x,
    waves,
    provisional,
    sent,
):
    odd, odd_z = _odd("gy"), _odd("gz")
    carrier = jnp.where(odd_z == 1, carrier_z[24:48], carrier_z[0:24])
    nothing = jnp.zeros((8, NX), F32)
    fields = []
    for q in range(3):
        layers = carrier * _dot(along_z[1 - odd_z], z_second[q])
        whole = partial[q] + carrier_y[...] * _dot(along_second[odd], y_second[q])
        low = whole[:24] + jnp.where(odd_z == 1, 0.0, layers)
        high = whole[CELLS - 24 :] + jnp.where(odd_z == 1, layers, 0.0)
        provisional[q] = jnp.concatenate([low, whole[24 : CELLS - 24], high], axis=0)
        rows = carrier_second[...] * _dot(along_rows[odd], y_second[q])
        fields.append(jnp.concatenate([rows, layers, nothing], axis=0))
    flux = [_split(f, 2) for f in _flux(metric, fields)]
    slope = _split(_dot(jnp.concatenate(flux[0], axis=1), along_x[...]), 2)
    high, low = (
        jnp.concatenate([flux[1][i], flux[2][i], slope[i]], axis=0) for i in range(2)
    )
    rows = _dot_nt(jnp.concatenate([high, high, low], axis=1), waves[...])
    more = lax.dot_general(
        jnp.concatenate(_split(rows, 2), axis=0),
        spread_rows[2 * odd + odd_z],
        (((0,), (0,)), ((), ())),
        preferred_element_type=F32,
    )
    for t in range(EXT // 128):
        at = slice(128 * t, 128 * t + 128)
        sent[:, 4 * t : 4 * t + 4, :] = (spectrum[:, at] + more[:, at]).reshape(DEV, 4, 128)


def plane_kernel(factors, got, outer, outer_back, twist, inner, inner_back, sent):
    chunks = EXT // 128
    parts = []
    for t in range(chunks):
        tr, ti = twist[0, :, 128 * t : 128 * t + 128], twist[1, :, 128 * t : 128 * t + 128]
        block = jnp.concatenate(
            [
                jnp.concatenate([got[:, 4 * t + 2 * c + part, :] for c in range(2)], axis=1)
                for part in range(2)
            ],
            axis=0,
        )
        high, low = _split(block, 2)
        block = _dot(outer[...], jnp.concatenate([high, high, low], axis=0))
        rows = []
        for c in range(2):
            at = slice(128 * c, 128 * c + 128)
            re, im = block[:DEV, at], block[DEV:, at]
            rows.append(jnp.concatenate([re * tr - im * ti, re * ti + im * tr], axis=1))
        high, low = _split(jnp.concatenate(rows, axis=0), 2)
        parts += [high, high, low]
    modes = _dot(jnp.concatenate(parts, axis=1), inner[...])
    solved = []
    for c in range(2):
        factor = factors[c]
        solved.append(modes[c * DEV : (c + 1) * DEV] * jnp.concatenate([factor, factor], axis=1))
    high, low = _split(jnp.concatenate(solved, axis=0), 2)
    left = jnp.concatenate([high] * 3 + [low] * 2, axis=1)
    every = _dot(left, inner_back[...])
    for t in range(chunks):
        tr, ti = twist[0, :, 128 * t : 128 * t + 128], twist[1, :, 128 * t : 128 * t + 128]
        cells = every[:, 256 * t : 256 * t + 256]
        columns = []
        for c in range(2):
            re, im = cells[c * DEV : (c + 1) * DEV, :128], cells[c * DEV : (c + 1) * DEV, 128:]
            columns.append(jnp.concatenate([re * tr + im * ti, im * tr - re * ti], axis=0))
        high, middle, low = _split(jnp.concatenate(columns, axis=1), 3)
        block = _dot(
            outer_back[...], jnp.concatenate([high] * 2 + [middle] * 2 + [low], axis=0)
        )
        for c in range(2):
            for part in range(2):
                sent[:, 4 * t + 2 * c + part, :] = block[
                    part * DEV : (part + 1) * DEV, 128 * c : 128 * c + 128
                ]


def project_kernel(
    metric,
    got,
    gather,
    keep,
    inverse,
    symbol,
    provisional,
    partial,
    carrier_y,
    carrier_z,
    y_first,
    y_second,
    z_first,
    z_second,
    along_first,
    along_second,
    along_z,
    motion,
    heat,
    held,
    held_heat,
    done,
):
    odd = _odd("gy")
    slopes = _dot(along_first[odd], y_first[0]) + _dot(along_second[odd], y_second[0])
    held_heat[...] = _with_z(
        partial[...] + carrier_y[...] * slopes, carrier_z, z_first[3], z_second[3], along_z
    )
    copies = [pltpu.make_async_copy(held_heat, heat, done.at[3])]
    copies[0].start()
    pushes = [[], [], []]
    for c in range(2):
        block = jnp.concatenate(
            [
                jnp.concatenate([got[:, 4 * t + 2 * c + part, :] for t in range(EXT // 128)], axis=1)
                for part in range(2)
            ],
            axis=0,
        )
        split = _split(block, 3)
        fields = _dot_nt(gather[...], jnp.concatenate(split, axis=1))
        along_y, along_z = fields[:CELLS], fields[CELLS:]
        own = _dot_nt(keep[...], jnp.concatenate([p[:, :CELLS] for p in split[:2]], axis=1))
        along_x = jnp.concatenate([-symbol[c] * own[:, 128:], symbol[c] * own[:, :128]], axis=1)
        for i in range(3):
            push = metric[i, 0] * along_x + metric[i, 1] * along_y + metric[i, 2] * along_z
            pushes[i].append(_split(push, 2))
    for i in range(3):
        (h0, l0), (h1, l1) = pushes[i]
        value = _dot(jnp.concatenate([h0, h0, h1, h1, l0, l1], axis=1), inverse[...])
        held[i] = provisional[i] - value
        copies.append(pltpu.make_async_copy(held.at[i], motion.at[i], done.at[i]))
        copies[-1].start()
    for copy in copies:
        copy.wait()


def _swaps(count):
    first = [(i, i ^ 1) for i in range(count)]
    second = [(i, (i + 1 if i % 2 else i - 1) % count) for i in range(count)]
    return first, second


def _step(state, metric, strain):
    along_y, along_z = _difference_matrices()
    forward, inverse, symbol = _x_tables()
    outer, twist, inner, inner_back, waves = _plane_tables()
    k = np.arange(NX // 2)
    wave_x = _kt(k, NX).astype(np.float32)
    wave_x[0] = 0.0
    circulant = _exact(_circulant_x())
    spread = _exact(-np.concatenate([along_y, along_y, along_z, along_z], axis=0).T)
    gather = _exact(np.concatenate([along_y, along_z], axis=0))
    keep = _exact(np.concatenate([np.eye(CELLS)] * 2, axis=1))
    gather = np.concatenate([gather] * 3, axis=1)
    below, above = along_y[:, CELLS : CELLS + 96], along_y[:, CELLS + 96 : CELLS + 192]
    beside_first = _exact(np.stack([above, below]))
    beside_second = _exact(np.stack([below, above]))
    rows = [[BY * w + y + i for w in range(BZ) for y in range(3)] for i in (0, BY - 3)]
    beside_rows = np.stack([beside_second[i][rows[i]] for i in range(2)])
    layers = [list(range(24)), list(range(CELLS - 24, CELLS))]
    spread_rows = []
    for i in range(4):
        chosen = rows[i // 2] + layers[i % 2]
        part = np.zeros((3, 128, EXT))
        for j, table in enumerate((-along_y, -along_z, np.eye(CELLS, EXT))):
            part[j, : len(chosen)] = table[chosen]
        spread_rows.append(np.concatenate([part.reshape(384, EXT)] * 2, axis=0))
    spread_rows = _exact(np.stack(spread_rows))
    beside_z = _exact(
        np.stack([along_z[CELLS - 24 :, CELLS + 216 : CELLS + 240], along_z[:24, CELLS + 192 : CELLS + 216]])
    )
    local = np.zeros((NX + CELLS, NX))
    local[:NX] = _circulant_x()
    local[NX:, :CELLS] = along_y[:, :CELLS]

    field = jax.ShapeDtypeStruct((CELLS, NX), F32)
    fields = lambda count: jax.ShapeDtypeStruct((count, CELLS, NX), F32)
    block = jax.ShapeDtypeStruct((DEV, 16, 128), F32)
    state = state.reshape(4, CELLS, NX)

    y_side = jax.ShapeDtypeStruct((3, 96, NX), BF16)
    y_side_heat = jax.ShapeDtypeStruct((1, 96, NX), BF16)
    z_side = jax.ShapeDtypeStruct((4, 24, NX), BF16)
    y_first, y_second, y_first_heat, y_second_heat, z_first, z_second = _call(
        edges_kernel,
        (y_side, y_side, y_side_heat, y_side_heat, z_side, z_side),
        [VMEM],
        "edges",
        20_000_000_000,
        64 * MIB,
        16,
    )(state)
    swaps_y, swaps_z = _swaps(GY), _swaps(GZ)
    y_first = lax.ppermute(y_first, "gy", swaps_y[0])
    y_second = lax.ppermute(y_second, "gy", swaps_y[1])
    z_first = lax.ppermute(z_first, "gz", swaps_z[0])
    z_second = lax.ppermute(z_second, "gz", swaps_z[1])
    partial, partial_heat, carrier_y, carrier_z, carrier_second, factors = _call(
        local_kernel,
        (
            fields(3),
            field,
            field,
            jax.ShapeDtypeStruct((48, NX), F32),
            jax.ShapeDtypeStruct((96, NX), F32),
            jax.ShapeDtypeStruct((2, DEV, CELLS), F32),
        ),
        [SMEM, SMEM, SMEM, VMEM, VMEM, VMEM],
        "local",
        1_000_000_000,
        4 * MIB,
        24,
    )(metric, strain, wave_x, state, _exact(local), waves)

    y_first_heat, y_second_heat, carrier_z = lax.optimization_barrier(
        (y_first_heat, y_second_heat, carrier_z)
    )
    y_first_heat = lax.ppermute(y_first_heat, "gy", swaps_y[0])
    y_second_heat = lax.ppermute(y_second_heat, "gy", swaps_y[1])
    circulant = np.concatenate([circulant, circulant], axis=0)
    forward = np.concatenate(_pieces(forward, 2)[[0, 1, 0]], axis=1)
    early, spectrum = _call(
        early_kernel,
        (fields(3), jax.ShapeDtypeStruct((NX, EXT), F32)),
        [SMEM] + [VMEM] * 10,
        "early",
        3_000_000_000,
        8 * MIB,
        20,
    )(
        metric,
        partial,
        carrier_y,
        carrier_z,
        y_first,
        z_first,
        beside_first,
        beside_z,
        spread,
        circulant,
        forward,
    )
    provisional, sent = _call(
        forward_kernel,
        (fields(3), block),
        [SMEM] + [VMEM] * 13,
        "forward",
        2_000_000_000,
        8 * MIB,
        20,
    )(
        metric,
        early,
        spectrum,
        carrier_y,
        carrier_z,
        carrier_second,
        y_second,
        z_second,
        beside_second,
        beside_rows,
        beside_z,
        spread_rows,
        circulant,
        forward,
    )
    sent, y_first_heat, y_second_heat = lax.optimization_barrier(
        (sent, y_first_heat, y_second_heat)
    )
    got = lax.all_to_all(sent, ("gy", "gz"), split_axis=0, concat_axis=0, tiled=True)
    sent = _call(
        plane_kernel, block, [VMEM] * 7, "plane", 3_600_000_000, 8 * MIB, 40
    )(
        factors,
        got,
        np.concatenate(_pieces(outer, 2)[[0, 1, 0]], axis=1),
        np.concatenate(_pieces(outer.T, 2)[[0, 1, 0, 1, 0]], axis=1),
        twist,
        inner,
        inner_back,
    )
    got = lax.all_to_all(sent, ("gy", "gz"), split_axis=0, concat_axis=0, tiled=True)
    motion, heat = _call(
        project_kernel,
        (fields(3), field),
        [SMEM] + [VMEM] * 16,
        "project",
        2_500_000_000,
        8 * MIB,
        40,
        out_specs=(ANY, ANY),
        scratch_shapes=[
            pltpu.VMEM((3, CELLS, NX), F32),
            pltpu.VMEM((CELLS, NX), F32),
            pltpu.SemaphoreType.DMA((4,)),
        ],
    )(
        metric,
        got,
        gather,
        keep,
        inverse,
        symbol,
        provisional,
        partial_heat,
        carrier_y,
        carrier_z,
        y_first_heat,
        y_second_heat,
        z_first,
        z_second,
        beside_first,
        beside_second,
        beside_z,
    )
    return motion.reshape(3, BZ, BY, NX), heat.reshape(BZ, BY, NX)


def solution(mesh):
    return jax.shard_map(
        _step,
        mesh=mesh,
        in_specs=(P(None, "gz", "gy", None), P(), P()),
        out_specs=(P(None, "gz", "gy", None), P("gz", "gy", None)),
        check_vma=False,
    )
```

```python
import numpy as np

import jax
import jax.numpy as jnp
import ml_dtypes
from jax import lax
from jax.experimental import pallas as pl
from jax.experimental.pallas import tpu as pltpu
from jax.sharding import PartitionSpec as P

F32 = jnp.float32
BF16 = jnp.bfloat16
NX, NY, NZ = 512, 256, 128
GY, GZ = 32, 4
BY, BZ = NY // GY, NZ // GZ
DEV = GY * GZ
CELLS = BY * BZ
EXT = 512
STEP = 0.4
COEF = {1: 45.0, -1: -45.0, 2: -9.0, -2: 9.0, 3: 1.0, -3: -1.0}
MIB = 1 << 20


def _pieces(table, count):
    rest = np.asarray(table, np.float64)
    out = []
    for _ in range(count):
        piece = rest.astype(np.float32).astype(ml_dtypes.bfloat16)
        out.append(piece)
        rest = rest - piece.astype(np.float64)
    return np.stack(out)


def _ext_cells():
    cells = [(w, y) for w in range(BZ) for y in range(BY)]
    cells += [(w, y) for w in range(BZ) for y in range(-3, 0)]
    cells += [(w, y) for w in range(BZ) for y in range(BY, BY + 3)]
    cells += [(w, y) for w in range(-3, 0) for y in range(BY)]
    cells += [(w, y) for w in range(BZ, BZ + 3) for y in range(BY)]
    return cells


def _difference_matrices():
    place = {cell: i for i, cell in enumerate(_ext_cells())}
    along_y = np.zeros((CELLS, EXT))
    along_z = np.zeros((CELLS, EXT))
    for w in range(BZ):
        for y in range(BY):
            row = place[(w, y)]
            for k, c in COEF.items():
                along_y[row, place[(w, y + k)]] = c
                along_z[row, place[(w + k, y)]] = c
    return along_y, along_z


def _circulant_x():
    table = np.zeros((NX, NX))
    for x in range(NX):
        for k, c in COEF.items():
            table[(x + k) % NX, x] = c
    return table


def _kt(modes, length):
    a = 2.0 * np.pi * modes / length
    return 1.5 * np.sin(a) - 0.3 * np.sin(2 * a) + np.sin(3 * a) / 30.0


def _x_tables():
    k = np.arange(NX // 2)[:, None]
    x = np.arange(NX)[None, :]
    angle = 2.0 * np.pi * ((k * x) % NX) / NX
    alternating = 1.0 - 2.0 * (np.arange(NX) % 2)
    forward = np.zeros((NX // 2, 2, NX))
    forward[:, 0], forward[:, 1] = np.cos(angle), -np.sin(angle)
    forward[0, 0], forward[0, 1] = 1.0, alternating
    inverse = 2.0 * forward
    inverse[0] = forward[0]
    inverse = inverse.reshape(DEV, 2, 2, NX).transpose(1, 2, 0, 3).reshape(2, 2 * DEV, NX)
    symbol = 60.0 * _kt(np.arange(NX // 2), NX)
    symbol[0] = 0.0
    symbol = symbol.reshape(DEV, 2).T.reshape(2, 1, DEV).astype(np.float32)
    inverse = _pieces(inverse / 60.0, 2)
    inverse = np.concatenate(
        [inverse[0, 0], inverse[1, 0], inverse[0, 1], inverse[1, 1], inverse[0, 0], inverse[0, 1]]
    )
    return forward.reshape(NX, NX) / 60.0, inverse, symbol


def _plane_tables():
    a = np.arange(DEV)
    m1, n1 = a // GZ, a % GZ
    gy, gz = a // GZ, a % GZ
    outer = np.exp(
        -2j * np.pi * (np.outer(m1, gy) / GY + np.outer(n1, gz) / GZ)
    )
    cells = np.array(_ext_cells())
    count = len(cells)
    w, y = cells[:, 0], cells[:, 1]
    twist = np.zeros((DEV, EXT), complex)
    twist[:, :count] = np.exp(-2j * np.pi * (np.outer(n1, w) / NZ + np.outer(m1, y) / NY))
    b = np.arange(CELLS)
    n2, m2 = b // BY, b % BY
    inner = np.zeros((EXT, CELLS), complex)
    inner[:count] = np.exp(-2j * np.pi * (np.outer(w, n2) / BZ + np.outer(y, m2) / BY))
    outer_real = np.block([[outer.real, -outer.imag], [outer.imag, outer.real]])
    inner_real = np.block([[inner.real, inner.imag], [-inner.imag, inner.real]])
    chunks = EXT // 128
    inner_back = _pieces(inner_real.T, 3)[[0, 1, 2, 0, 1]].reshape(5, 2 * CELLS, 2, chunks, 128)
    inner_back = inner_back.transpose(0, 1, 3, 2, 4).reshape(10 * CELLS, 1024)
    inner_real = _pieces(inner_real, 2)[[0, 1, 0]].reshape(3, 2, chunks, 128, 2 * CELLS)
    inner_real = inner_real.transpose(2, 0, 1, 3, 4).reshape(chunks * 768, 2 * CELLS)
    mode_y = m1[:, None] + GY * m2[None, :]
    mode_z = n1[:, None] + GZ * n2[None, :]
    edge = (((2 * mode_y) % NY == 0) & ((2 * mode_z) % NZ == 0)).astype(np.float32)
    waves = np.stack([_kt(mode_y, NY), _kt(mode_z, NZ), edge]).astype(np.float32)
    twist = np.stack([twist.real, twist.imag]).astype(np.float32)
    return outer_real, twist, inner_real, inner_back, waves


def _exact(table):
    return np.asarray(table, np.float32).astype(ml_dtypes.bfloat16)


def _dot(left, right):
    return lax.dot_general(left, right, (((1,), (0,)), ((), ())), preferred_element_type=F32)


def _dot_nt(left, right):
    return lax.dot_general(left, right, (((1,), (1,)), ((), ())), preferred_element_type=F32)


def _split(value, count):
    out = []
    for i in range(count):
        piece = value.astype(BF16)
        out.append(piece)
        if i + 1 < count:
            value = value - piece.astype(F32)
    return out


VMEM = pl.BlockSpec(memory_space=pltpu.VMEM)
SMEM = pl.BlockSpec(memory_space=pltpu.SMEM)
ANY = pl.BlockSpec(memory_space=pl.ANY)


def _call(kernel, out_shape, in_specs, name, flops, nbytes, vmem, scratch_shapes=(), out_specs=None):
    return pl.pallas_call(
        kernel,
        out_shape=out_shape,
        in_specs=in_specs,
        out_specs=out_specs or jax.tree.map(lambda _: VMEM, out_shape),
        scratch_shapes=scratch_shapes,
        compiler_params=pltpu.CompilerParams(vmem_limit_bytes=vmem * MIB),
        cost_estimate=pl.CostEstimate(flops=flops, bytes_accessed=nbytes, transcendentals=0),
        name=name,
    )


def _odd(axis):
    return lax.rem(lax.axis_index(axis), 2)


def edges_kernel(state, y_first, y_second, y_first_heat, y_second_heat, z_first, z_second):
    odd_y, odd_z = _odd("gy"), _odd("gz")
    row = lax.broadcasted_iota(jnp.int32, (240, CELLS), 0)
    column = lax.broadcasted_iota(jnp.int32, (240, CELLS), 1)
    second = row >= 96
    within = jnp.where(second, row - 96, row)
    third = (within * 171) >> 9
    top_y = (BY - 3) * jnp.where(second, odd_y, 1 - odd_y)
    along_y = BY * third + (within - 3 * third) + top_y
    second = row >= 216
    top_z = (CELLS - 24) * jnp.where(second, odd_z, 1 - odd_z)
    along_z = jnp.where(second, row - 216, row - 192) + top_z
    source = jnp.where(row >= 192, along_z, along_y)
    pick = jnp.where(column == source, 1.0, 0.0).astype(BF16)
    for q in range(4):
        rows = _dot(pick, state[q])
        first, second, at = (y_first, y_second, q) if q < 3 else (y_first_heat, y_second_heat, 0)
        first[at] = rows[0:96].astype(BF16)
        second[at] = rows[96:192].astype(BF16)
        z_first[q] = rows[192:216].astype(BF16)
        z_second[q] = rows[216:240].astype(BF16)


def local_kernel(
    metric, strain, wave_x, state, along, waves, partial, partial_heat, carrier_y, carrier_z, carrier_second, factors
):
    along_x, along_y = along[:NX], along[NX:, :CELLS]
    speeds = [state[q].astype(F32) for q in range(4)]
    contra = [
        metric[0, j] * speeds[0] + metric[1, j] * speeds[1] + metric[2, j] * speeds[2]
        for j in range(3)
    ]
    scale = -STEP / 60.0
    carrier_y[...] = scale * contra[1]
    row = lax.broadcasted_iota(jnp.int32, (96, CELLS), 0)
    column = lax.broadcasted_iota(jnp.int32, (96, CELLS), 1)
    third = (row * 171) >> 9
    source = BY * third + (row - 3 * third) + (BY - 3) * _odd("gy")
    pick = jnp.where(column == source, 1.0, 0.0).astype(BF16)
    high, middle, low = _split(scale * contra[1], 3)
    carrier_second[...] = (_dot(pick, low) + _dot(pick, middle)) + _dot(pick, high)
    carrier_z[0:24] = scale * contra[2][0:24]
    carrier_z[24:48] = scale * contra[2][CELLS - 24 :]
    nothing = jnp.zeros((24, NX), F32)
    for q in range(4):
        d_x = _dot(state[q], along_x)
        d_y = _dot(along_y, state[q])
        tall = jnp.concatenate([nothing, speeds[q], nothing], axis=0)

        def moved(k):
            return tall[(3 + k) * BY : (3 + k) * BY + CELLS]

        d_z = (
            45.0 * (moved(1) - moved(-1)) - 9.0 * (moved(2) - moved(-2)) + (moved(3) - moved(-3))
        )
        carried = contra[0] * d_x + contra[1] * d_y + contra[2] * d_z
        if q < 3:
            rest = strain[q, 0] * speeds[0] + strain[q, 1] * speeds[1] + strain[q, 2] * speeds[2]
            if q == 2:
                rest = rest - speeds[3]
        else:
            rest = speeds[2]
        value = speeds[q] + scale * carried - STEP * rest
        if q < 3:
            partial[q] = value
        else:
            partial_heat[...] = value
    here = lax.axis_index("gy") * GZ + lax.axis_index("gz")
    wave_y, wave_z, edge = waves[0], waves[1], waves[2]
    for c in range(2):
        wx = wave_x[2 * here + c]
        symbol = jnp.zeros((DEV, CELLS), F32)
        for i in range(3):
            mixed = metric[i, 0] * wx + metric[i, 1] * wave_y + metric[i, 2] * wave_z
            symbol = symbol + mixed * mixed
        out = (edge * jnp.where(2 * here + c == 0, 1.0, 0.0)) > 0.5
        factors[c] = jnp.where(
            out, 0.0, -1.0 / (jnp.where(out, 1.0, symbol) * float(NX * NY * NZ))
        )


def _with_z(whole, carrier_z, z_first, z_second, along_z):
    odd = _odd("gz")
    first, second = _dot(along_z[odd], z_first), _dot(along_z[1 - odd], z_second)
    below = jnp.where(odd == 1, first, second)
    above = jnp.where(odd == 1, second, first)
    low = whole[:24] + carrier_z[0:24] * below
    high = whole[CELLS - 24 :] + carrier_z[24:48] * above
    return jnp.concatenate([low, whole[24 : CELLS - 24], high], axis=0)


def _flux(metric, fields):
    return [
        metric[0, j] * fields[0] + metric[1, j] * fields[1] + metric[2, j] * fields[2]
        for j in range(3)
    ]


def early_kernel(
    metric,
    partial,
    carrier_y,
    carrier_z,
    y_first,
    z_first,
    along_first,
    along_z,
    spread,
    along_x,
    waves,
    provisional,
    spectrum,
):
    odd, odd_z = _odd("gy"), _odd("gz")
    fields = []
    for q in range(3):
        whole = partial[q] + carrier_y[...] * _dot(along_first[odd], y_first[q])
        first = _dot(along_z[odd_z], z_first[q])
        low = whole[:24] + carrier_z[0:24] * jnp.where(odd_z == 1, first, 0.0)
        high = whole[CELLS - 24 :] + carrier_z[24:48] * jnp.where(odd_z == 1, 0.0, first)
        fields.append(jnp.concatenate([low, whole[24 : CELLS - 24], high], axis=0))
        provisional[q] = fields[q]
    flux = [_split(f, 2) for f in _flux(metric, fields)]
    stacked = [jnp.concatenate(flux[j], axis=0) for j in (1, 2)]
    own = _dot(jnp.concatenate(flux[0], axis=1), along_x[...])
    for part in range(EXT // CELLS):
        if part == 0:
            block = own + _dot(spread[:CELLS], jnp.concatenate(stacked, axis=0))
        else:
            beside_y = _dot(spread[CELLS : CELLS + 192, :NX], stacked[0])
            beside_z = _dot(spread[CELLS + 192 :, NX:], stacked[1])
            block = jnp.concatenate([beside_y, beside_z], axis=0)
        high, low = _split(block, 2)
        spectrum[:, part * CELLS : (part + 1) * CELLS] = _dot_nt(
            waves[...], jnp.concatenate([high, high, low], axis=1)
        )


def forward_kernel(
    metric,
    partial,
    spectrum,
    carrier_y,
    carrier_z,
    carrier_second,
    y_second,
    z_second,
    along_second,
    along_rows,
    along_z,
    spread_rows,
    along_x,
    waves,
    provisional,
    sent,
):
    odd, odd_z = _odd("gy"), _odd("gz")
    carrier = jnp.where(odd_z == 1, carrier_z[24:48], carrier_z[0:24])
    nothing = jnp.zeros((8, NX), F32)
    fields = []
    for q in range(3):
        layers = carrier * _dot(along_z[1 - odd_z], z_second[q])
        whole = partial[q] + carrier_y[...] * _dot(along_second[odd], y_second[q])
        low = whole[:24] + jnp.where(odd_z == 1, 0.0, layers)
        high = whole[CELLS - 24 :] + jnp.where(odd_z == 1, layers, 0.0)
        provisional[q] = jnp.concatenate([low, whole[24 : CELLS - 24], high], axis=0)
        rows = carrier_second[...] * _dot(along_rows[odd], y_second[q])
        fields.append(jnp.concatenate([rows, layers, nothing], axis=0))
    flux = [_split(f, 2) for f in _flux(metric, fields)]
    slope = _split(_dot(jnp.concatenate(flux[0], axis=1), along_x[...]), 2)
    high, low = (
        jnp.concatenate([flux[1][i], flux[2][i], slope[i]], axis=0) for i in range(2)
    )
    rows = _dot_nt(jnp.concatenate([high, high, low], axis=1), waves[...])
    more = lax.dot_general(
        jnp.concatenate(_split(rows, 2), axis=0),
        spread_rows[2 * odd + odd_z],
        (((0,), (0,)), ((), ())),
        preferred_element_type=F32,
    )
    for t in range(EXT // 128):
        at = slice(128 * t, 128 * t + 128)
        sent[:, 4 * t : 4 * t + 4, :] = (spectrum[:, at] + more[:, at]).reshape(DEV, 4, 128)


def plane_kernel(factors, got, outer, outer_back, twist, inner, inner_back, sent):
    chunks = EXT // 128
    parts = []
    for t in range(chunks):
        tr, ti = twist[0, :, 128 * t : 128 * t + 128], twist[1, :, 128 * t : 128 * t + 128]
        block = jnp.concatenate(
            [
                jnp.concatenate([got[:, 4 * t + 2 * c + part, :] for c in range(2)], axis=1)
                for part in range(2)
            ],
            axis=0,
        )
        high, low = _split(block, 2)
        block = _dot(outer[...], jnp.concatenate([high, high, low], axis=0))
        rows = []
        for c in range(2):
            at = slice(128 * c, 128 * c + 128)
            re, im = block[:DEV, at], block[DEV:, at]
            rows.append(jnp.concatenate([re * tr - im * ti, re * ti + im * tr], axis=1))
        high, low = _split(jnp.concatenate(rows, axis=0), 2)
        parts += [high, high, low]
    modes = _dot(jnp.concatenate(parts, axis=1), inner[...])
    solved = []
    for c in range(2):
        factor = factors[c]
        solved.append(modes[c * DEV : (c + 1) * DEV] * jnp.concatenate([factor, factor], axis=1))
    high, low = _split(jnp.concatenate(solved, axis=0), 2)
    left = jnp.concatenate([high] * 3 + [low] * 2, axis=1)
    every = _dot(left, inner_back[...])
    for t in range(chunks):
        tr, ti = twist[0, :, 128 * t : 128 * t + 128], twist[1, :, 128 * t : 128 * t + 128]
        cells = every[:, 256 * t : 256 * t + 256]
        columns = []
        for c in range(2):
            re, im = cells[c * DEV : (c + 1) * DEV, :128], cells[c * DEV : (c + 1) * DEV, 128:]
            columns.append(jnp.concatenate([re * tr + im * ti, im * tr - re * ti], axis=0))
        high, middle, low = _split(jnp.concatenate(columns, axis=1), 3)
        block = _dot(
            outer_back[...], jnp.concatenate([high] * 2 + [middle] * 2 + [low], axis=0)
        )
        for c in range(2):
            for part in range(2):
                sent[:, 4 * t + 2 * c + part, :] = block[
                    part * DEV : (part + 1) * DEV, 128 * c : 128 * c + 128
                ]


def project_kernel(
    metric,
    got,
    gather,
    keep,
    inverse,
    symbol,
    provisional,
    partial,
    carrier_y,
    carrier_z,
    y_first,
    y_second,
    z_first,
    z_second,
    along_first,
    along_second,
    along_z,
    motion,
    heat,
    held,
    held_heat,
    done,
):
    odd = _odd("gy")
    slopes = _dot(along_first[odd], y_first[0]) + _dot(along_second[odd], y_second[0])
    held_heat[...] = _with_z(
        partial[...] + carrier_y[...] * slopes, carrier_z, z_first[3], z_second[3], along_z
    )
    copies = [pltpu.make_async_copy(held_heat, heat, done.at[3])]
    copies[0].start()
    pushes = [[], [], []]
    for c in range(2):
        block = jnp.concatenate(
            [
                jnp.concatenate([got[:, 4 * t + 2 * c + part, :] for t in range(EXT // 128)], axis=1)
                for part in range(2)
            ],
            axis=0,
        )
        split = _split(block, 3)
        fields = _dot_nt(gather[...], jnp.concatenate(split, axis=1))
        along_y, along_z = fields[:CELLS], fields[CELLS:]
        own = _dot_nt(keep[...], jnp.concatenate([p[:, :CELLS] for p in split[:2]], axis=1))
        along_x = jnp.concatenate([-symbol[c] * own[:, 128:], symbol[c] * own[:, :128]], axis=1)
        for i in range(3):
            push = metric[i, 0] * along_x + metric[i, 1] * along_y + metric[i, 2] * along_z
            pushes[i].append(_split(push, 2))
    for i in range(3):
        (h0, l0), (h1, l1) = pushes[i]
        value = _dot(jnp.concatenate([h0, h0, h1, h1, l0, l1], axis=1), inverse[...])
        held[i] = provisional[i] - value
        copies.append(pltpu.make_async_copy(held.at[i], motion.at[i], done.at[i]))
        copies[-1].start()
    for copy in copies:
        copy.wait()


def _swaps(count):
    first = [(i, i ^ 1) for i in range(count)]
    second = [(i, (i + 1 if i % 2 else i - 1) % count) for i in range(count)]
    return first, second


def _step(state, metric, strain):
    along_y, along_z = _difference_matrices()
    forward, inverse, symbol = _x_tables()
    outer, twist, inner, inner_back, waves = _plane_tables()
    k = np.arange(NX // 2)
    wave_x = _kt(k, NX).astype(np.float32)
    wave_x[0] = 0.0
    circulant = _exact(_circulant_x())
    spread = _exact(-np.concatenate([along_y, along_y, along_z, along_z], axis=0).T)
    gather = _exact(np.concatenate([along_y, along_z], axis=0))
    keep = _exact(np.concatenate([np.eye(CELLS)] * 2, axis=1))
    gather = np.concatenate([gather] * 3, axis=1)
    below, above = along_y[:, CELLS : CELLS + 96], along_y[:, CELLS + 96 : CELLS + 192]
    beside_first = _exact(np.stack([above, below]))
    beside_second = _exact(np.stack([below, above]))
    rows = [[BY * w + y + i for w in range(BZ) for y in range(3)] for i in (0, BY - 3)]
    beside_rows = np.stack([beside_second[i][rows[i]] for i in range(2)])
    layers = [list(range(24)), list(range(CELLS - 24, CELLS))]
    spread_rows = []
    for i in range(4):
        chosen = rows[i // 2] + layers[i % 2]
        part = np.zeros((3, 128, EXT))
        for j, table in enumerate((-along_y, -along_z, np.eye(CELLS, EXT))):
            part[j, : len(chosen)] = table[chosen]
        spread_rows.append(np.concatenate([part.reshape(384, EXT)] * 2, axis=0))
    spread_rows = _exact(np.stack(spread_rows))
    beside_z = _exact(
        np.stack([along_z[CELLS - 24 :, CELLS + 216 : CELLS + 240], along_z[:24, CELLS + 192 : CELLS + 216]])
    )
    local = np.zeros((NX + CELLS, NX))
    local[:NX] = _circulant_x()
    local[NX:, :CELLS] = along_y[:, :CELLS]

    field = jax.ShapeDtypeStruct((CELLS, NX), F32)
    fields = lambda count: jax.ShapeDtypeStruct((count, CELLS, NX), F32)
    block = jax.ShapeDtypeStruct((DEV, 16, 128), F32)
    state = state.reshape(4, CELLS, NX)

    y_side = jax.ShapeDtypeStruct((3, 96, NX), BF16)
    y_side_heat = jax.ShapeDtypeStruct((1, 96, NX), BF16)
    z_side = jax.ShapeDtypeStruct((4, 24, NX), BF16)
    y_first, y_second, y_first_heat, y_second_heat, z_first, z_second = _call(
        edges_kernel,
        (y_side, y_side, y_side_heat, y_side_heat, z_side, z_side),
        [VMEM],
        "edges",
        20_000_000_000,
        64 * MIB,
        16,
    )(state)
    swaps_y, swaps_z = _swaps(GY), _swaps(GZ)
    y_first = lax.ppermute(y_first, "gy", swaps_y[0])
    y_second = lax.ppermute(y_second, "gy", swaps_y[1])
    z_first = lax.ppermute(z_first, "gz", swaps_z[0])
    partial, partial_heat, carrier_y, carrier_z, carrier_second, factors = _call(
        local_kernel,
        (
            fields(3),
            field,
            field,
            jax.ShapeDtypeStruct((48, NX), F32),
            jax.ShapeDtypeStruct((96, NX), F32),
            jax.ShapeDtypeStruct((2, DEV, CELLS), F32),
        ),
        [SMEM, SMEM, SMEM, VMEM, VMEM, VMEM],
        "local",
        1_000_000_000,
        4 * MIB,
        24,
    )(metric, strain, wave_x, state, _exact(local), waves)

    z_second, y_first_heat, y_second_heat, carrier_z = lax.optimization_barrier(
        (z_second, y_first_heat, y_second_heat, carrier_z)
    )
    z_second = lax.ppermute(z_second, "gz", swaps_z[1])
    y_first_heat = lax.ppermute(y_first_heat, "gy", swaps_y[0])
    y_second_heat = lax.ppermute(y_second_heat, "gy", swaps_y[1])
    circulant = np.concatenate([circulant, circulant], axis=0)
    forward = np.concatenate(_pieces(forward, 2)[[0, 1, 0]], axis=1)
    early, spectrum = _call(
        early_kernel,
        (fields(3), jax.ShapeDtypeStruct((NX, EXT), F32)),
        [SMEM] + [VMEM] * 10,
        "early",
        3_000_000_000,
        8 * MIB,
        20,
    )(
        metric,
        partial,
        carrier_y,
        carrier_z,
        y_first,
        z_first,
        beside_first,
        beside_z,
        spread,
        circulant,
        forward,
    )
    provisional, sent = _call(
        forward_kernel,
        (fields(3), block),
        [SMEM] + [VMEM] * 13,
        "forward",
        2_000_000_000,
        8 * MIB,
        20,
    )(
        metric,
        early,
        spectrum,
        carrier_y,
        carrier_z,
        carrier_second,
        y_second,
        z_second,
        beside_second,
        beside_rows,
        beside_z,
        spread_rows,
        circulant,
        forward,
    )
    sent, y_first_heat, y_second_heat = lax.optimization_barrier(
        (sent, y_first_heat, y_second_heat)
    )
    got = lax.all_to_all(sent, ("gy", "gz"), split_axis=0, concat_axis=0, tiled=True)
    sent = _call(
        plane_kernel, block, [VMEM] * 7, "plane", 3_600_000_000, 8 * MIB, 40
    )(
        factors,
        got,
        np.concatenate(_pieces(outer, 2)[[0, 1, 0]], axis=1),
        np.concatenate(_pieces(outer.T, 2)[[0, 1, 0, 1, 0]], axis=1),
        twist,
        inner,
        inner_back,
    )
    got = lax.all_to_all(sent, ("gy", "gz"), split_axis=0, concat_axis=0, tiled=True)
    motion, heat = _call(
        project_kernel,
        (fields(3), field),
        [SMEM] + [VMEM] * 16,
        "project",
        2_500_000_000,
        8 * MIB,
        40,
        out_specs=(ANY, ANY),
        scratch_shapes=[
            pltpu.VMEM((3, CELLS, NX), F32),
            pltpu.VMEM((CELLS, NX), F32),
            pltpu.SemaphoreType.DMA((4,)),
        ],
    )(
        metric,
        got,
        gather,
        keep,
        inverse,
        symbol,
        provisional,
        partial_heat,
        carrier_y,
        carrier_z,
        y_first_heat,
        y_second_heat,
        z_first,
        z_second,
        beside_first,
        beside_second,
        beside_z,
    )
    return motion.reshape(3, BZ, BY, NX), heat.reshape(BZ, BY, NX)


def solution(mesh):
    return jax.shard_map(
        _step,
        mesh=mesh,
        in_specs=(P(None, "gz", "gy", None), P(), P()),
        out_specs=(P(None, "gz", "gy", None), P("gz", "gy", None)),
        check_vma=False,
    )
```

```python
import numpy as np

import jax
import jax.numpy as jnp
import ml_dtypes
from jax import lax
from jax.experimental import pallas as pl
from jax.experimental.pallas import tpu as pltpu
from jax.sharding import PartitionSpec as P

F32 = jnp.float32
BF16 = jnp.bfloat16
NX, NY, NZ = 512, 256, 128
GY, GZ = 32, 4
BY, BZ = NY // GY, NZ // GZ
DEV = GY * GZ
CELLS = BY * BZ
EXT = 512
STEP = 0.4
COEF = {1: 45.0, -1: -45.0, 2: -9.0, -2: 9.0, 3: 1.0, -3: -1.0}
MIB = 1 << 20


def _pieces(table, count):
    rest = np.asarray(table, np.float64)
    out = []
    for _ in range(count):
        piece = rest.astype(np.float32).astype(ml_dtypes.bfloat16)
        out.append(piece)
        rest = rest - piece.astype(np.float64)
    return np.stack(out)


def _ext_cells():
    cells = [(w, y) for w in range(BZ) for y in range(BY)]
    cells += [(w, y) for w in range(BZ) for y in range(-3, 0)]
    cells += [(w, y) for w in range(BZ) for y in range(BY, BY + 3)]
    cells += [(w, y) for w in range(-3, 0) for y in range(BY)]
    cells += [(w, y) for w in range(BZ, BZ + 3) for y in range(BY)]
    return cells


def _difference_matrices():
    place = {cell: i for i, cell in enumerate(_ext_cells())}
    along_y = np.zeros((CELLS, EXT))
    along_z = np.zeros((CELLS, EXT))
    for w in range(BZ):
        for y in range(BY):
            row = place[(w, y)]
            for k, c in COEF.items():
                along_y[row, place[(w, y + k)]] = c
                along_z[row, place[(w + k, y)]] = c
    return along_y, along_z


def _circulant_x():
    table = np.zeros((NX, NX))
    for x in range(NX):
        for k, c in COEF.items():
            table[(x + k) % NX, x] = c
    return table


def _kt(modes, length):
    a = 2.0 * np.pi * modes / length
    return 1.5 * np.sin(a) - 0.3 * np.sin(2 * a) + np.sin(3 * a) / 30.0


def _x_tables():
    k = np.arange(NX // 2)[:, None]
    x = np.arange(NX)[None, :]
    angle = 2.0 * np.pi * ((k * x) % NX) / NX
    alternating = 1.0 - 2.0 * (np.arange(NX) % 2)
    forward = np.zeros((NX // 2, 2, NX))
    forward[:, 0], forward[:, 1] = np.cos(angle), -np.sin(angle)
    forward[0, 0], forward[0, 1] = 1.0, alternating
    inverse = 2.0 * forward
    inverse[0] = forward[0]
    inverse = inverse.reshape(DEV, 2, 2, NX).transpose(1, 2, 0, 3).reshape(2, 2 * DEV, NX)
    symbol = 60.0 * _kt(np.arange(NX // 2), NX)
    symbol[0] = 0.0
    symbol = symbol.reshape(DEV, 2).T.reshape(2, 1, DEV).astype(np.float32)
    inverse = _pieces(inverse / 60.0, 2)
    inverse = np.concatenate(
        [inverse[0, 0], inverse[1, 0], inverse[0, 1], inverse[1, 1], inverse[0, 0], inverse[0, 1]]
    )
    return forward.reshape(NX, NX) / 60.0, inverse, symbol


def _plane_tables():
    a = np.arange(DEV)
    m1, n1 = a // GZ, a % GZ
    gy, gz = a // GZ, a % GZ
    outer = np.exp(
        -2j * np.pi * (np.outer(m1, gy) / GY + np.outer(n1, gz) / GZ)
    )
    cells = np.array(_ext_cells())
    count = len(cells)
    w, y = cells[:, 0], cells[:, 1]
    twist = np.zeros((DEV, EXT), complex)
    twist[:, :count] = np.exp(-2j * np.pi * (np.outer(n1, w) / NZ + np.outer(m1, y) / NY))
    b = np.arange(CELLS)
    n2, m2 = b // BY, b % BY
    inner = np.zeros((EXT, CELLS), complex)
    inner[:count] = np.exp(-2j * np.pi * (np.outer(w, n2) / BZ + np.outer(y, m2) / BY))
    outer_real = np.block([[outer.real, -outer.imag], [outer.imag, outer.real]])
    inner_real = np.block([[inner.real, inner.imag], [-inner.imag, inner.real]])
    chunks = EXT // 128
    inner_back = _pieces(inner_real.T, 3)[[0, 1, 2, 0, 1]].reshape(5, 2 * CELLS, 2, chunks, 128)
    inner_back = inner_back.transpose(0, 1, 3, 2, 4).reshape(10 * CELLS, 1024)
    inner_real = _pieces(inner_real, 2)[[0, 1, 0]].reshape(3, 2, chunks, 128, 2 * CELLS)
    inner_real = inner_real.transpose(2, 0, 1, 3, 4).reshape(chunks * 768, 2 * CELLS)
    mode_y = m1[:, None] + GY * m2[None, :]
    mode_z = n1[:, None] + GZ * n2[None, :]
    edge = (((2 * mode_y) % NY == 0) & ((2 * mode_z) % NZ == 0)).astype(np.float32)
    waves = np.stack([_kt(mode_y, NY), _kt(mode_z, NZ), edge]).astype(np.float32)
    twist = np.stack([twist.real, twist.imag]).astype(np.float32)
    return outer_real, twist, inner_real, inner_back, waves


def _exact(table):
    return np.asarray(table, np.float32).astype(ml_dtypes.bfloat16)


def _dot(left, right):
    return lax.dot_general(left, right, (((1,), (0,)), ((), ())), preferred_element_type=F32)


def _dot_nt(left, right):
    return lax.dot_general(left, right, (((1,), (1,)), ((), ())), preferred_element_type=F32)


def _split(value, count):
    out = []
    for i in range(count):
        piece = value.astype(BF16)
        out.append(piece)
        if i + 1 < count:
            value = value - piece.astype(F32)
    return out


VMEM = pl.BlockSpec(memory_space=pltpu.VMEM)
SMEM = pl.BlockSpec(memory_space=pltpu.SMEM)
ANY = pl.BlockSpec(memory_space=pl.ANY)


def _call(kernel, out_shape, in_specs, name, flops, nbytes, vmem, scratch_shapes=(), out_specs=None):
    return pl.pallas_call(
        kernel,
        out_shape=out_shape,
        in_specs=in_specs,
        out_specs=out_specs or jax.tree.map(lambda _: VMEM, out_shape),
        scratch_shapes=scratch_shapes,
        compiler_params=pltpu.CompilerParams(vmem_limit_bytes=vmem * MIB),
        cost_estimate=pl.CostEstimate(flops=flops, bytes_accessed=nbytes, transcendentals=0),
        name=name,
    )


def _odd(axis):
    return lax.rem(lax.axis_index(axis), 2)


def first_kernel(state, y_first):
    row = lax.broadcasted_iota(jnp.int32, (96, CELLS), 0)
    column = lax.broadcasted_iota(jnp.int32, (96, CELLS), 1)
    third = (row * 171) >> 9
    source = BY * third + (row - 3 * third) + (BY - 3) * (1 - _odd("gy"))
    pick = jnp.where(column == source, 1.0, 0.0).astype(BF16)
    for q in range(3):
        y_first[q] = _dot(pick, state[q]).astype(BF16)


def edges_kernel(state, y_second, y_first_heat, y_second_heat, z_first, z_second):
    odd_y, odd_z = _odd("gy"), _odd("gz")
    row = lax.broadcasted_iota(jnp.int32, (240, CELLS), 0)
    column = lax.broadcasted_iota(jnp.int32, (240, CELLS), 1)
    second = row >= 96
    within = jnp.where(second, row - 96, row)
    third = (within * 171) >> 9
    top_y = (BY - 3) * jnp.where(second, odd_y, 1 - odd_y)
    along_y = BY * third + (within - 3 * third) + top_y
    second = row >= 216
    top_z = (CELLS - 24) * jnp.where(second, odd_z, 1 - odd_z)
    along_z = jnp.where(second, row - 216, row - 192) + top_z
    source = jnp.where(row >= 192, along_z, along_y)
    pick = jnp.where(column == source, 1.0, 0.0).astype(BF16)
    for q in range(4):
        rows = _dot(pick, state[q])
        if q < 3:
            y_second[q] = rows[96:192].astype(BF16)
        else:
            y_first_heat[0] = rows[0:96].astype(BF16)
            y_second_heat[0] = rows[96:192].astype(BF16)
        z_first[q] = rows[192:216].astype(BF16)
        z_second[q] = rows[216:240].astype(BF16)


def local_kernel(
    metric, strain, wave_x, state, along, waves, partial, partial_heat, carrier_y, carrier_z, carrier_second, factors
):
    along_x, along_y = along[:NX], along[NX:, :CELLS]
    speeds = [state[q].astype(F32) for q in range(4)]
    contra = [
        metric[0, j] * speeds[0] + metric[1, j] * speeds[1] + metric[2, j] * speeds[2]
        for j in range(3)
    ]
    scale = -STEP / 60.0
    carrier_y[...] = scale * contra[1]
    row = lax.broadcasted_iota(jnp.int32, (96, CELLS), 0)
    column = lax.broadcasted_iota(jnp.int32, (96, CELLS), 1)
    third = (row * 171) >> 9
    source = BY * third + (row - 3 * third) + (BY - 3) * _odd("gy")
    pick = jnp.where(column == source, 1.0, 0.0).astype(BF16)
    high, middle, low = _split(scale * contra[1], 3)
    carrier_second[...] = (_dot(pick, low) + _dot(pick, middle)) + _dot(pick, high)
    carrier_z[0:24] = scale * contra[2][0:24]
    carrier_z[24:48] = scale * contra[2][CELLS - 24 :]
    nothing = jnp.zeros((24, NX), F32)
    for q in range(4):
        d_x = _dot(state[q], along_x)
        d_y = _dot(along_y, state[q])
        tall = jnp.concatenate([nothing, speeds[q], nothing], axis=0)

        def moved(k):
            return tall[(3 + k) * BY : (3 + k) * BY + CELLS]

        d_z = (
            45.0 * (moved(1) - moved(-1)) - 9.0 * (moved(2) - moved(-2)) + (moved(3) - moved(-3))
        )
        carried = contra[0] * d_x + contra[1] * d_y + contra[2] * d_z
        if q < 3:
            rest = strain[q, 0] * speeds[0] + strain[q, 1] * speeds[1] + strain[q, 2] * speeds[2]
            if q == 2:
                rest = rest - speeds[3]
        else:
            rest = speeds[2]
        value = speeds[q] + scale * carried - STEP * rest
        if q < 3:
            partial[q] = value
        else:
            partial_heat[...] = value
    here = lax.axis_index("gy") * GZ + lax.axis_index("gz")
    wave_y, wave_z, edge = waves[0], waves[1], waves[2]
    for c in range(2):
        wx = wave_x[2 * here + c]
        symbol = jnp.zeros((DEV, CELLS), F32)
        for i in range(3):
            mixed = metric[i, 0] * wx + metric[i, 1] * wave_y + metric[i, 2] * wave_z
            symbol = symbol + mixed * mixed
        out = (edge * jnp.where(2 * here + c == 0, 1.0, 0.0)) > 0.5
        factors[c] = jnp.where(
            out, 0.0, -1.0 / (jnp.where(out, 1.0, symbol) * float(NX * NY * NZ))
        )


def _with_z(whole, carrier_z, z_first, z_second, along_z):
    odd = _odd("gz")
    first, second = _dot(along_z[odd], z_first), _dot(along_z[1 - odd], z_second)
    below = jnp.where(odd == 1, first, second)
    above = jnp.where(odd == 1, second, first)
    low = whole[:24] + carrier_z[0:24] * below
    high = whole[CELLS - 24 :] + carrier_z[24:48] * above
    return jnp.concatenate([low, whole[24 : CELLS - 24], high], axis=0)


def _flux(metric, fields):
    return [
        metric[0, j] * fields[0] + metric[1, j] * fields[1] + metric[2, j] * fields[2]
        for j in range(3)
    ]


def early_kernel(
    metric,
    partial,
    carrier_y,
    carrier_z,
    y_first,
    z_first,
    along_first,
    along_z,
    spread,
    along_x,
    waves,
    provisional,
    spectrum,
):
    odd, odd_z = _odd("gy"), _odd("gz")
    fields = []
    for q in range(3):
        whole = partial[q] + carrier_y[...] * _dot(along_first[odd], y_first[q])
        first = _dot(along_z[odd_z], z_first[q])
        low = whole[:24] + carrier_z[0:24] * jnp.where(odd_z == 1, first, 0.0)
        high = whole[CELLS - 24 :] + carrier_z[24:48] * jnp.where(odd_z == 1, 0.0, first)
        fields.append(jnp.concatenate([low, whole[24 : CELLS - 24], high], axis=0))
        provisional[q] = fields[q]
    flux = [_split(f, 2) for f in _flux(metric, fields)]
    stacked = [jnp.concatenate(flux[j], axis=0) for j in (1, 2)]
    own = _dot(jnp.concatenate(flux[0], axis=1), along_x[...])
    for part in range(EXT // CELLS):
        if part == 0:
            block = own + _dot(spread[:CELLS], jnp.concatenate(stacked, axis=0))
        else:
            beside_y = _dot(spread[CELLS : CELLS + 192, :NX], stacked[0])
            beside_z = _dot(spread[CELLS + 192 :, NX:], stacked[1])
            block = jnp.concatenate([beside_y, beside_z], axis=0)
        high, low = _split(block, 2)
        spectrum[:, part * CELLS : (part + 1) * CELLS] = _dot_nt(
            waves[...], jnp.concatenate([high, high, low], axis=1)
        )


def forward_kernel(
    metric,
    partial,
    spectrum,
    carrier_y,
    carrier_z,
    carrier_second,
    y_second,
    z_second,
    along_second,
    along_rows,
    along_z,
    spread_rows,
    along_x,
    waves,
    provisional,
    sent,
):
    odd, odd_z = _odd("gy"), _odd("gz")
    carrier = jnp.where(odd_z == 1, carrier_z[24:48], carrier_z[0:24])
    nothing = jnp.zeros((8, NX), F32)
    fields = []
    for q in range(3):
        layers = carrier * _dot(along_z[1 - odd_z], z_second[q])
        whole = partial[q] + carrier_y[...] * _dot(along_second[odd], y_second[q])
        low = whole[:24] + jnp.where(odd_z == 1, 0.0, layers)
        high = whole[CELLS - 24 :] + jnp.where(odd_z == 1, layers, 0.0)
        provisional[q] = jnp.concatenate([low, whole[24 : CELLS - 24], high], axis=0)
        rows = carrier_second[...] * _dot(along_rows[odd], y_second[q])
        fields.append(jnp.concatenate([rows, layers, nothing], axis=0))
    flux = [_split(f, 2) for f in _flux(metric, fields)]
    slope = _split(_dot(jnp.concatenate(flux[0], axis=1), along_x[...]), 2)
    high, low = (
        jnp.concatenate([flux[1][i], flux[2][i], slope[i]], axis=0) for i in range(2)
    )
    rows = _dot_nt(jnp.concatenate([high, high, low], axis=1), waves[...])
    more = lax.dot_general(
        jnp.concatenate(_split(rows, 2), axis=0),
        spread_rows[2 * odd + odd_z],
        (((0,), (0,)), ((), ())),
        preferred_element_type=F32,
    )
    for t in range(EXT // 128):
        at = slice(128 * t, 128 * t + 128)
        sent[:, 4 * t : 4 * t + 4, :] = (spectrum[:, at] + more[:, at]).reshape(DEV, 4, 128)


def plane_kernel(factors, got, outer, outer_back, twist, inner, inner_back, sent):
    chunks = EXT // 128
    parts = []
    for t in range(chunks):
        tr, ti = twist[0, :, 128 * t : 128 * t + 128], twist[1, :, 128 * t : 128 * t + 128]
        block = jnp.concatenate(
            [
                jnp.concatenate([got[:, 4 * t + 2 * c + part, :] for c in range(2)], axis=1)
                for part in range(2)
            ],
            axis=0,
        )
        high, low = _split(block, 2)
        block = _dot(outer[...], jnp.concatenate([high, high, low], axis=0))
        rows = []
        for c in range(2):
            at = slice(128 * c, 128 * c + 128)
            re, im = block[:DEV, at], block[DEV:, at]
            rows.append(jnp.concatenate([re * tr - im * ti, re * ti + im * tr], axis=1))
        high, low = _split(jnp.concatenate(rows, axis=0), 2)
        parts += [high, high, low]
    modes = _dot(jnp.concatenate(parts, axis=1), inner[...])
    solved = []
    for c in range(2):
        factor = factors[c]
        solved.append(modes[c * DEV : (c + 1) * DEV] * jnp.concatenate([factor, factor], axis=1))
    high, low = _split(jnp.concatenate(solved, axis=0), 2)
    left = jnp.concatenate([high] * 3 + [low] * 2, axis=1)
    every = _dot(left, inner_back[...])
    for t in range(chunks):
        tr, ti = twist[0, :, 128 * t : 128 * t + 128], twist[1, :, 128 * t : 128 * t + 128]
        cells = every[:, 256 * t : 256 * t + 256]
        columns = []
        for c in range(2):
            re, im = cells[c * DEV : (c + 1) * DEV, :128], cells[c * DEV : (c + 1) * DEV, 128:]
            columns.append(jnp.concatenate([re * tr + im * ti, im * tr - re * ti], axis=0))
        high, middle, low = _split(jnp.concatenate(columns, axis=1), 3)
        block = _dot(
            outer_back[...], jnp.concatenate([high] * 2 + [middle] * 2 + [low], axis=0)
        )
        for c in range(2):
            for part in range(2):
                sent[:, 4 * t + 2 * c + part, :] = block[
                    part * DEV : (part + 1) * DEV, 128 * c : 128 * c + 128
                ]


def project_kernel(
    metric,
    got,
    gather,
    keep,
    inverse,
    symbol,
    provisional,
    partial,
    carrier_y,
    carrier_z,
    y_first,
    y_second,
    z_first,
    z_second,
    along_first,
    along_second,
    along_z,
    motion,
    heat,
    held,
    held_heat,
    done,
):
    odd = _odd("gy")
    slopes = _dot(along_first[odd], y_first[0]) + _dot(along_second[odd], y_second[0])
    held_heat[...] = _with_z(
        partial[...] + carrier_y[...] * slopes, carrier_z, z_first[3], z_second[3], along_z
    )
    copies = [pltpu.make_async_copy(held_heat, heat, done.at[3])]
    copies[0].start()
    pushes = [[], [], []]
    for c in range(2):
        block = jnp.concatenate(
            [
                jnp.concatenate([got[:, 4 * t + 2 * c + part, :] for t in range(EXT // 128)], axis=1)
                for part in range(2)
            ],
            axis=0,
        )
        split = _split(block, 3)
        fields = _dot_nt(gather[...], jnp.concatenate(split, axis=1))
        along_y, along_z = fields[:CELLS], fields[CELLS:]
        own = _dot_nt(keep[...], jnp.concatenate([p[:, :CELLS] for p in split[:2]], axis=1))
        along_x = jnp.concatenate([-symbol[c] * own[:, 128:], symbol[c] * own[:, :128]], axis=1)
        for i in range(3):
            push = metric[i, 0] * along_x + metric[i, 1] * along_y + metric[i, 2] * along_z
            pushes[i].append(_split(push, 2))
    for i in range(3):
        (h0, l0), (h1, l1) = pushes[i]
        value = _dot(jnp.concatenate([h0, h0, h1, h1, l0, l1], axis=1), inverse[...])
        held[i] = provisional[i] - value
        copies.append(pltpu.make_async_copy(held.at[i], motion.at[i], done.at[i]))
        copies[-1].start()
    for copy in copies:
        copy.wait()


def _swaps(count):
    first = [(i, i ^ 1) for i in range(count)]
    second = [(i, (i + 1 if i % 2 else i - 1) % count) for i in range(count)]
    return first, second


def _step(state, metric, strain):
    along_y, along_z = _difference_matrices()
    forward, inverse, symbol = _x_tables()
    outer, twist, inner, inner_back, waves = _plane_tables()
    k = np.arange(NX // 2)
    wave_x = _kt(k, NX).astype(np.float32)
    wave_x[0] = 0.0
    circulant = _exact(_circulant_x())
    spread = _exact(-np.concatenate([along_y, along_y, along_z, along_z], axis=0).T)
    gather = _exact(np.concatenate([along_y, along_z], axis=0))
    keep = _exact(np.concatenate([np.eye(CELLS)] * 2, axis=1))
    gather = np.concatenate([gather] * 3, axis=1)
    below, above = along_y[:, CELLS : CELLS + 96], along_y[:, CELLS + 96 : CELLS + 192]
    beside_first = _exact(np.stack([above, below]))
    beside_second = _exact(np.stack([below, above]))
    rows = [[BY * w + y + i for w in range(BZ) for y in range(3)] for i in (0, BY - 3)]
    beside_rows = np.stack([beside_second[i][rows[i]] for i in range(2)])
    layers = [list(range(24)), list(range(CELLS - 24, CELLS))]
    spread_rows = []
    for i in range(4):
        chosen = rows[i // 2] + layers[i % 2]
        part = np.zeros((3, 128, EXT))
        for j, table in enumerate((-along_y, -along_z, np.eye(CELLS, EXT))):
            part[j, : len(chosen)] = table[chosen]
        spread_rows.append(np.concatenate([part.reshape(384, EXT)] * 2, axis=0))
    spread_rows = _exact(np.stack(spread_rows))
    beside_z = _exact(
        np.stack([along_z[CELLS - 24 :, CELLS + 216 : CELLS + 240], along_z[:24, CELLS + 192 : CELLS + 216]])
    )
    local = np.zeros((NX + CELLS, NX))
    local[:NX] = _circulant_x()
    local[NX:, :CELLS] = along_y[:, :CELLS]

    field = jax.ShapeDtypeStruct((CELLS, NX), F32)
    fields = lambda count: jax.ShapeDtypeStruct((count, CELLS, NX), F32)
    block = jax.ShapeDtypeStruct((DEV, 16, 128), F32)
    state = state.reshape(4, CELLS, NX)

    y_side = jax.ShapeDtypeStruct((3, 96, NX), BF16)
    y_side_heat = jax.ShapeDtypeStruct((1, 96, NX), BF16)
    z_side = jax.ShapeDtypeStruct((4, 24, NX), BF16)
    y_first = _call(first_kernel, y_side, [VMEM], "first", 100_000_000, 2 * MIB, 16)(state)
    y_second, y_first_heat, y_second_heat, z_first, z_second = _call(
        edges_kernel,
        (y_side, y_side_heat, y_side_heat, z_side, z_side),
        [VMEM],
        "edges",
        20_000_000_000,
        64 * MIB,
        16,
    )(state)
    swaps_y, swaps_z = _swaps(GY), _swaps(GZ)
    y_first = lax.ppermute(y_first, "gy", swaps_y[0])
    y_second = lax.ppermute(y_second, "gy", swaps_y[1])
    z_first = lax.ppermute(z_first, "gz", swaps_z[0])
    z_second = lax.ppermute(z_second, "gz", swaps_z[1])
    partial, partial_heat, carrier_y, carrier_z, carrier_second, factors = _call(
        local_kernel,
        (
            fields(3),
            field,
            field,
            jax.ShapeDtypeStruct((48, NX), F32),
            jax.ShapeDtypeStruct((96, NX), F32),
            jax.ShapeDtypeStruct((2, DEV, CELLS), F32),
        ),
        [SMEM, SMEM, SMEM, VMEM, VMEM, VMEM],
        "local",
        1_000_000_000,
        4 * MIB,
        24,
    )(metric, strain, wave_x, state, _exact(local), waves)

    y_first_heat, y_second_heat, carrier_z = lax.optimization_barrier(
        (y_first_heat, y_second_heat, carrier_z)
    )
    y_first_heat = lax.ppermute(y_first_heat, "gy", swaps_y[0])
    y_second_heat = lax.ppermute(y_second_heat, "gy", swaps_y[1])
    circulant = np.concatenate([circulant, circulant], axis=0)
    forward = np.concatenate(_pieces(forward, 2)[[0, 1, 0]], axis=1)
    early, spectrum = _call(
        early_kernel,
        (fields(3), jax.ShapeDtypeStruct((NX, EXT), F32)),
        [SMEM] + [VMEM] * 10,
        "early",
        3_000_000_000,
        8 * MIB,
        20,
    )(
        metric,
        partial,
        carrier_y,
        carrier_z,
        y_first,
        z_first,
        beside_first,
        beside_z,
        spread,
        circulant,
        forward,
    )
    provisional, sent = _call(
        forward_kernel,
        (fields(3), block),
        [SMEM] + [VMEM] * 13,
        "forward",
        2_000_000_000,
        8 * MIB,
        20,
    )(
        metric,
        early,
        spectrum,
        carrier_y,
        carrier_z,
        carrier_second,
        y_second,
        z_second,
        beside_second,
        beside_rows,
        beside_z,
        spread_rows,
        circulant,
        forward,
    )
    sent, y_first_heat, y_second_heat = lax.optimization_barrier(
        (sent, y_first_heat, y_second_heat)
    )
    got = lax.all_to_all(sent, ("gy", "gz"), split_axis=0, concat_axis=0, tiled=True)
    sent = _call(
        plane_kernel, block, [VMEM] * 7, "plane", 3_600_000_000, 8 * MIB, 40
    )(
        factors,
        got,
        np.concatenate(_pieces(outer, 2)[[0, 1, 0]], axis=1),
        np.concatenate(_pieces(outer.T, 2)[[0, 1, 0, 1, 0]], axis=1),
        twist,
        inner,
        inner_back,
    )
    got = lax.all_to_all(sent, ("gy", "gz"), split_axis=0, concat_axis=0, tiled=True)
    motion, heat = _call(
        project_kernel,
        (fields(3), field),
        [SMEM] + [VMEM] * 16,
        "project",
        2_500_000_000,
        8 * MIB,
        40,
        out_specs=(ANY, ANY),
        scratch_shapes=[
            pltpu.VMEM((3, CELLS, NX), F32),
            pltpu.VMEM((CELLS, NX), F32),
            pltpu.SemaphoreType.DMA((4,)),
        ],
    )(
        metric,
        got,
        gather,
        keep,
        inverse,
        symbol,
        provisional,
        partial_heat,
        carrier_y,
        carrier_z,
        y_first_heat,
        y_second_heat,
        z_first,
        z_second,
        beside_first,
        beside_second,
        beside_z,
    )
    return motion.reshape(3, BZ, BY, NX), heat.reshape(BZ, BY, NX)


def solution(mesh):
    return jax.shard_map(
        _step,
        mesh=mesh,
        in_specs=(P(None, "gz", "gy", None), P(), P()),
        out_specs=(P(None, "gz", "gy", None), P("gz", "gy", None)),
        check_vma=False,
    )
```
